128 devices in a mesh: les: 8 (over z_lo, y), ac: 16 (over x, z_hi, core).
Axes of the slice: x: 4, y: 4, z: 4 (z_hi: 2, z_lo: 2; z = z_hi * 2 + z_lo), core: 2. Of those that a mesh axis runs over, the one named last changes fastest.
Arguments:
- velocity: bfloat16 [3, 131072, 128], P(None, ('les', 'ac')), may hold values from -6 to 6
- vorticity: bfloat16 [3, 131072, 128], P(None, ('les', 'ac')), may hold values from -6 to 6
- cover: int32 [131072, 2], P(('les', 'ac')), may hold values from 0 to 127, all different within a row; in each aligned block of 1024 rows (0 to 1023, 1024 to 2047, ...) at most 32 rows name the same one
- target_line: int32 [131072, 2], P(('les', 'ac')), may hold values from 0 to 511
- phase: int32 [131072, 2], P(('les', 'ac')), may hold values from 0 to 3
- fringe_lines: int32 [128, 2], P(('les', 'ac')), may hold values from 0 to 511
- acoustic: float32 [4, 65536, 256], P(None, ('les', 'ac')), may hold values from -6 to 6
Outputs:
- acoustic_next: float32 [4, 65536, 256], P(None, ('les', 'ac'))
The draws below stay inside these ranges and needn't reach their ends.
Inputs may be any that keep to these rules, and one draw needn't show every extreme that they name: `cover`: within the rows of one device, no acoustic block is named more than 32 times, and some block exactly 32 times; the 2 blocks of one slab differ.
All inputs are finite; a program needn't handle non-finite values.
Results may differ from the reference program's by a relative error of at most 0.003.
Values may be sent and summed in bfloat16 or wider, within the bound.
No kernel may reach another device: no remote copies, remote signals or barrier semaphores. Data moves between devices by JAX's collectives and lax.ppermute only.
A program may use at most 64 MiB of HBM per device.

```python
import math
import jax
import jax.numpy as jnp
import numpy as np
from jax import lax

SLAB_CELLS = 128
CELLS = 256
NOFF = 4
TOP = 2
SLAB_DEV = 1024
LINES = 512
SLABS = 131072
NBLK = 128
CAP = 32
ROWS = 65536
N_LES = 8
N_AC = 16


def touch_ends(array, rng, low, top_value):
    place = [jax.random.randint(jax.random.fold_in(rng, axis), (), 0, length) for axis, length in enumerate(array.shape)]
    longest = array.shape.index(max(array.shape))
    next_to = place[:longest] + [(place[longest] + 1) % array.shape[longest]] + place[longest + 1:]
    return array.at[tuple(place)].set(low).at[tuple(next_to)].set(top_value)


def steps_of(rng, dims, shards, smallest, top_value):
    level, own = 1.0, jax.random.fold_in(rng, 6)
    for axis_at, shards_of in shards:
        steps = jnp.exp(jax.random.uniform(jax.random.fold_in(own, axis_at), (shards_of,), jnp.float32, smallest / len(shards), top_value / len(shards)))
        level = level * jnp.repeat(steps, dims[axis_at] // shards_of).reshape([-1 if axis == axis_at else 1 for axis in range(len(dims))])
    return level


def assign_block(stream_key, own, number, rows, count, top, reach, skew):
    ranking = jax.random.permutation(stream_key, count)
    crowded, ordinary = portions_of(count, rows * top, reach, skew, True), portions_of(count, rows * top, reach, skew, False)
    places = jnp.arange(count)

    def named(sizes, turn):
        used = int((sizes > 0).sum())
        fixed = max(1, used // 4)
        moved = fixed + (places - fixed + turn * (used - fixed)) % max(1, count - fixed)
        return jnp.zeros((count,), jnp.int32).at[ranking[jnp.where(places < fixed, places, moved)]].set(jnp.asarray(sizes, jnp.int32))

    sizes = jnp.where(number % 4 == 0, named(crowded, number // 4), named(ordinary, number - number // 4 - 1))
    mixed = jax.random.permutation(jax.random.fold_in(own, 3), count)
    giver, receiver = mixed[0:count // 2 * 2:2], mixed[1:count // 2 * 2:2]
    room = jnp.minimum(sizes[giver] - 1, reach - sizes[receiver]) // 2
    room = jnp.where((giver == ranking[0]) | (receiver == ranking[0]) | (sizes[receiver] == 0), 0, jnp.maximum(room, 0))
    moved = jax.random.randint(jax.random.fold_in(own, 4), (count // 2,), 0, 1 << 20) % (room + 1)
    sizes = sizes.at[giver].add(-moved).at[receiver].add(moved)
    labels = jnp.searchsorted(jnp.cumsum(sizes), jnp.arange(rows * top), side="right").astype(jnp.int32)
    table = labels.reshape(top, rows).T
    table = table[jax.random.permutation(jax.random.fold_in(own, 1), rows)]
    turn = jax.random.randint(jax.random.fold_in(own, 2), (rows, 1), 0, top)
    return jnp.take_along_axis(table, (jnp.arange(top)[None, :] + turn) % top, axis=1)


def portions_of(amount, total, limit, skew, full):
    portions = [(1 << 20) // math.isqrt(grade ** skew) + 1 for grade in range(1, amount + 1)]
    largest = limit if full else min(limit, max(-(-total // amount), total * portions[0] // sum(portions)))
    least = 1 if total - largest >= amount - 1 else 0
    counts, rest = [largest] + [least] * (amount - 1), total - largest - least * (amount - 1)
    while rest > 0:
        movable = [i for i in range(1, amount) if counts[i] < largest] or [i for i in range(1, amount) if counts[i] < limit]
        pool, left = sum([portions[i] for i in movable]), rest
        for i in movable:
            addition = min(limit - counts[i], max(1, left * portions[i] // pool), rest)
            counts[i] = counts[i] + addition
            rest = rest - addition
    return np.array(counts)


def noise(key, shape, deviation, reach, shards=(), held_as=jnp.bfloat16):
    array = jax.random.normal(key, shape, jnp.float32) * deviation
    if len(shards) > 0:
        array = steps_of(key, shape, shards, -0.22, 0.18) * array
    return jnp.clip(array, min=-reach, max=reach).astype(held_as)


def setup_inputs(seed: int = 0) -> dict:
    key_of = jax.random.split(jax.random.key(seed), 8)
    velocity = noise(key_of[0], (3, SLABS, SLAB_CELLS), 1.0, 6.0, ((1, 128),))
    vorticity = noise(key_of[1], (3, SLABS, SLAB_CELLS), 1.0, 6.0, ((1, 128),))
    cover_keys = jax.random.split(jax.random.fold_in(key_of[2], 1), SLABS // SLAB_DEV)
    cover_turns = jax.random.permutation(jax.random.fold_in(key_of[2], 3), SLABS // SLAB_DEV)
    cover = jax.vmap(lambda own, number: assign_block(jax.random.fold_in(key_of[2], 2), own, number, SLAB_DEV, NBLK, TOP, CAP, 2))(cover_keys, cover_turns).reshape((SLABS, TOP))
    target_line = touch_ends(jax.random.randint(key_of[3], (SLABS, TOP), 0, LINES), jax.random.fold_in(key_of[3], 1), 0, LINES - 1).astype(jnp.int32)
    phase = touch_ends(jax.random.randint(key_of[4], (SLABS, TOP), 0, NOFF), jax.random.fold_in(key_of[4], 1), 0, NOFF - 1).astype(jnp.int32)
    fringe_lines = touch_ends(jax.random.randint(key_of[5], (NBLK, 2), 0, LINES), jax.random.fold_in(key_of[5], 1), 0, LINES - 1).astype(jnp.int32)
    acoustic = noise(key_of[6], (4, ROWS, CELLS), 1.0, 6.0, ((1, 128),), jnp.float32)
    return {"velocity": velocity, "vorticity": vorticity, "cover": cover, "target_line": target_line, "phase": phase, "fringe_lines": fringe_lines, "acoustic": acoustic}


ADVECT = 0.5
STEP = 0.4

def lagrange_table(coarse, fine, phases):
    fine_ids = jnp.arange(fine, dtype=jnp.int32)
    phase_ids = jnp.arange(phases, dtype=jnp.int32)
    numerator = phases * fine_ids[None, :] + phase_ids[:, None]
    first_tap = jnp.clip(numerator // (2 * phases) - 1, 0, coarse - 4)
    where_x = numerator.astype(jnp.float32) / (2.0 * phases)
    coarse_ids = jnp.arange(coarse, dtype=jnp.int32)
    lagrange = jnp.zeros((phases, coarse, fine), jnp.float32)
    for tap_index in range(4):
        weight = jnp.ones_like(where_x)
        for other_tap in range(4):
            if other_tap != tap_index:
                weight = weight * (where_x - (first_tap + other_tap).astype(jnp.float32)) / float(tap_index - other_tap)
        hit_mask = coarse_ids[None, :, None] == (first_tap + tap_index)[:, None, :]
        lagrange = lagrange + jnp.where(hit_mask, weight[:, None, :], jnp.float32(0.0))
    return lagrange

def derivative_matrix(cells):
    cell_ids = np.arange(cells)
    distance = cell_ids[:, None] - cell_ids[None, :]
    rhs_matrix = jnp.asarray(np.where(distance == -1, 0.75, np.where(distance == 1, -0.75, 0.0)), dtype=jnp.float32)
    main_band = jnp.ones((cells,), jnp.float32)
    lower_band = jnp.asarray(np.where(cell_ids == 0, 0.0, 0.25), dtype=jnp.float32)
    upper_band = jnp.asarray(np.where(cell_ids == cells - 1, 0.0, 0.25), dtype=jnp.float32)
    solved = lax.linalg.tridiagonal_solve(lower_band, main_band, upper_band, rhs_matrix)
    return solved.T

def ape_rates(dx_all, dy_pressure, dy_across, source):
    pressure = -ADVECT * dx_all[0] - dx_all[1] - dy_across
    along = -ADVECT * dx_all[1] - dx_all[0] - source[0]
    across = -ADVECT * dx_all[2] - dy_pressure - source[1]
    spanwise = -ADVECT * dx_all[3] - source[2]
    return jnp.stack([pressure, along, across, spanwise])

def reference(velocity, vorticity, cover, target_line, phase, fringe_lines, acoustic):
    lamb = jnp.cross(vorticity.astype(jnp.float32), velocity.astype(jnp.float32), axis=0).astype(jnp.bfloat16)
    slab_rows = jnp.transpose(lamb, (1, 0, 2)).reshape(SLABS, 3 * SLAB_CELLS)
    weights = lagrange_table(SLAB_CELLS, CELLS, NOFF).astype(jnp.bfloat16)

    def add_block(total, block_index):
        start = (block_index * SLAB_DEV).astype(jnp.int32)
        rows_here = lax.dynamic_slice_in_dim(slab_rows, start, SLAB_DEV, 0).astype(jnp.float32)
        blocks_here = lax.dynamic_slice_in_dim(cover, start, SLAB_DEV, 0)
        lines_here = lax.dynamic_slice_in_dim(target_line, start, SLAB_DEV, 0)
        phases_here = lax.dynamic_slice_in_dim(phase, start, SLAB_DEV, 0)
        for column in range(TOP):
            segment = (blocks_here[:, column] * LINES + lines_here[:, column]) * NOFF + phases_here[:, column]
            total = total.at[segment].add(rows_here)
        return (total, None)
    initial = jnp.zeros((NBLK * LINES * NOFF, 3 * SLAB_CELLS), jnp.float32)
    total, _ = lax.scan(add_block, initial, jnp.arange(SLABS // SLAB_DEV, dtype=jnp.int32))
    gathered = total.astype(jnp.bfloat16).reshape(NBLK * LINES, NOFF, 3, SLAB_CELLS)
    source_flat = jnp.einsum('rock,okj->crj', gathered.astype(jnp.float32), weights.astype(jnp.float32))
    source = source_flat.reshape(3, N_LES, N_AC, LINES, CELLS)
    dmat = derivative_matrix(CELLS)
    fringe = fringe_lines.reshape(N_LES, N_AC, 2)

    def face_of(field, column):
        index_grid = jnp.broadcast_to(fringe[:, :, column][:, :, None, None], (N_LES, N_AC, 1, CELLS))
        return jnp.take_along_axis(field, index_grid, axis=2)[:, :, 0, :]

    def y_rate(field, column_up, column_down):
        up_face = face_of(field, column_up)
        down_face = face_of(field, column_down)
        zero_face = jnp.zeros_like(up_face[:, :1])
        low_ghost = jnp.concatenate([zero_face, up_face[:, :-1]], axis=1)
        high_ghost = jnp.concatenate([down_face[:, 1:], zero_face], axis=1)
        extended = jnp.concatenate([low_ghost[:, :, None], field, high_ghost[:, :, None]], axis=2)
        return (extended[:, :, 2:] - extended[:, :, :-2]) * 0.5

    def tendency(state):
        dx_all = jnp.dot(state.reshape(-1, CELLS), dmat, precision=lax.Precision.HIGHEST).reshape(state.shape)
        dy_pressure = y_rate(state[0], 0, 1)
        dy_across = y_rate(state[2], 0, 1)
        return ape_rates(dx_all, dy_pressure, dy_across, source)
    state = acoustic.reshape(4, N_LES, N_AC, LINES, CELLS)
    first = tendency(state)
    second = tendency(state + 0.5 * STEP * first)
    third = tendency(state + 0.5 * STEP * second)
    fourth = tendency(state + STEP * third)
    result = state + STEP / 6.0 * (first + 2.0 * second + 2.0 * third + fourth)
    return result.reshape(4, ROWS, CELLS)
```

```python
import functools

import jax
import jax.numpy as jnp
import numpy as np
from jax import lax
from jax.experimental import pallas as pl
from jax.experimental.pallas import tpu as pltpu
from jax.sharding import PartitionSpec as P

PHASES = 4
ADVECT = 0.5
STEP = 0.4
AXES = ("les", "ac")
CODE_ROWS = 8
GROUP = 16
MIB = 1 << 20


def lagrange_weights(coarse, fine):
    table = np.zeros((PHASES, coarse, fine), np.float32)
    for phase in range(PHASES):
        numerator = PHASES * np.arange(fine) + phase
        first_tap = np.clip(numerator // (2 * PHASES) - 1, 0, coarse - 4)
        where_x = numerator.astype(np.float32) / np.float32(2 * PHASES)
        for tap in range(4):
            weight = np.ones((fine,), np.float32)
            for other in range(4):
                if other != tap:
                    gap = where_x - (first_tap + other).astype(np.float32)
                    weight = weight * gap / np.float32(tap - other)
            table[phase, first_tap + tap, np.arange(fine)] += weight
    return table.reshape(PHASES * coarse, fine)


def derivative_matrix(cells):
    off = np.eye(cells, k=1)
    a = np.eye(cells) + 0.25 * (off + off.T)
    b = 0.75 * (off - off.T)
    return np.linalg.solve(a, b).T


def whole(count):
    return [pl.BlockSpec(memory_space=pltpu.VMEM)] * count


def scalars():
    return pl.BlockSpec(memory_space=pltpu.SMEM)


def f32(x):
    return x.astype(jnp.float32)


def pack_kernel(place, velocity, vorticity, cover, line, phase, payload, table, ranks):
    devices = payload.shape[0]
    slabs = velocity.shape[1]
    coarse = velocity.shape[2]
    capacity = (payload.shape[1] - CODE_ROWS) // 3
    for c in range(3):
        a, b = (c + 1) % 3, (c + 2) % 3
        lamb = f32(vorticity[a]) * f32(velocity[b]) - f32(vorticity[b]) * f32(velocity[a])
        table[:, c * coarse:(c + 1) * coarse] = lamb.astype(jnp.bfloat16)
    cov = cover[...]
    code = line[...] * PHASES + phase[...]
    high = f32((code // 8) * 8)
    low = f32(code % 8)
    row8 = lax.broadcasted_iota(jnp.int32, (128, slabs), 0)
    facts = jnp.where(row8 == 0, high[0:1], 0.0)
    facts = jnp.where(row8 == 1, low[0:1], facts)
    facts = jnp.where(row8 == 2, high[1:2], facts)
    facts = jnp.where(row8 == 3, low[1:2], facts)
    facts = jnp.where(row8 == 4, f32(cov[0:1]), facts)
    table[:, 3 * coarse:] = facts.T.astype(jnp.bfloat16)

    ids = lax.broadcasted_iota(jnp.int32, (devices, slabs), 0)
    hit = (cov[0:1] == ids) | (cov[1:2] == ids)
    hit_f = jnp.where(hit, 1.0, 0.0)
    width = 256
    earlier = (
        lax.broadcasted_iota(jnp.int32, (width, width), 0)
        < lax.broadcasted_iota(jnp.int32, (width, width), 1)
    )
    earlier = jnp.where(earlier, 1.0, 0.0).astype(jnp.bfloat16)
    before = jnp.zeros((devices, 1), jnp.float32)
    for k in range(slabs // width):
        part = hit_f[:, k * width:(k + 1) * width]
        rank = jnp.dot(part.astype(jnp.bfloat16), earlier, preferred_element_type=jnp.float32)
        ranks[:, k * width:(k + 1) * width] = jnp.where(part > 0.0, rank + before, -1.0)
        before = before + jnp.sum(part, axis=1, keepdims=True)

    slot = f32(lax.broadcasted_iota(jnp.int32, (GROUP, capacity, slabs), 1))
    span = GROUP * capacity
    lane_owner = lax.broadcasted_iota(jnp.int32, (1, span), 1) // capacity
    own_lanes = (
        lax.broadcasted_iota(jnp.int32, (GROUP, span), 1) // capacity
        == lax.broadcasted_iota(jnp.int32, (GROUP, span), 0)
    )
    my_part = lax.broadcasted_iota(jnp.int32, (GROUP, 128), 1) // capacity == place[0]
    which_row = lax.broadcasted_iota(jnp.int32, (GROUP, CODE_ROWS, 128), 1)

    def spread(values):
        rows = jnp.where(own_lanes, jnp.broadcast_to(values, (GROUP, span)), 0.0)
        total = rows[:, :128]
        for k in range(1, span // 128):
            total = total + rows[:, k * 128:(k + 1) * 128]
        shift = 64
        while shift >= capacity:
            total = total + pltpu.roll(total, shift, 1)
            shift //= 2
        return jnp.where(my_part, total, 0.0)[:, None, :]

    def group(g, carry):
        first = pl.multiple_of(g * GROUP, GROUP)
        mine = ranks[pl.ds(first, GROUP), :]
        choose = jnp.where(mine[:, None, :] == slot, 1.0, 0.0)
        choose = choose.reshape(span, slabs).astype(jnp.bfloat16)
        picked = jnp.dot(choose, table[...], preferred_element_type=jnp.float32)
        for c in range(3):
            rows = picked[:, c * coarse:(c + 1) * coarse].reshape(GROUP, capacity, coarse)
            payload[pl.ds(first, GROUP), c * capacity:(c + 1) * capacity, :] = rows.astype(
                jnp.bfloat16
            )
        codes = picked[:, 3 * coarse:].T
        is_first = codes[4:5] == f32(lane_owner + first)
        upper = spread(jnp.where(is_first, codes[0:1], codes[2:3]))
        lower = spread(jnp.where(is_first, codes[1:2], codes[3:4]))
        tile = jnp.where(which_row == 0, upper, jnp.where(which_row == 1, lower, 0.0))
        payload[pl.ds(first, GROUP), 3 * capacity:, :] = tile.astype(jnp.bfloat16)
        return carry

    lax.fori_loop(0, devices // GROUP, group, 0)


def pack(place, velocity, vorticity, cover, line, phase, devices, capacity):
    _, slabs, coarse = velocity.shape
    return pl.pallas_call(
        pack_kernel,
        out_shape=jax.ShapeDtypeStruct((devices, 3 * capacity + CODE_ROWS, coarse), jnp.bfloat16),
        in_specs=[scalars()] + whole(5),
        out_specs=whole(1)[0],
        scratch_shapes=[
            pltpu.VMEM((slabs, 3 * coarse + 128), jnp.bfloat16),
            pltpu.VMEM((devices, slabs), jnp.float32),
        ],
        compiler_params=pltpu.CompilerParams(vmem_limit_bytes=32 * MIB),
        name="pack",
    )(place, velocity, vorticity, cover, line, phase)


def split(x):
    high = x.astype(jnp.bfloat16)
    return high, (x - f32(high)).astype(jnp.bfloat16)


def dx(field, dmat):
    high, low = split(field)
    cells = field.shape[-1]
    both = jnp.dot(high, dmat[...], preferred_element_type=jnp.float32)
    return (
        both[:, :cells]
        + both[:, cells:]
        + jnp.dot(low, dmat[:, :cells], preferred_element_type=jnp.float32)
    )


def dy(field, low_row, high_row):
    lines = field.shape[0]
    at = lax.broadcasted_iota(jnp.int32, field.shape, 0)
    above = jnp.where(at == lines - 1, high_row, pltpu.roll(field, lines - 1, 0))
    below = jnp.where(at == 0, low_row, pltpu.roll(field, 1, 0))
    return (above - below) * 0.5


def homogeneous(state, low_ghost, high_ghost, dmat):
    dx_p, dx_u = dx(state[0], dmat), dx(state[1], dmat)
    yield 0, -ADVECT * dx_p - dx_u - dy(state[2], low_ghost[1:2], high_ghost[1:2])
    yield 1, -ADVECT * dx_u - dx_p
    yield 2, -ADVECT * dx(state[2], dmat) - dy(state[0], low_ghost[0:1], high_ghost[0:1])
    yield 3, -ADVECT * dx(state[3], dmat)


def faces_of(fringe, fields, up, down):
    for n, c in enumerate((0, 2)):
        up[n:n + 1, :] = fields[c, pl.ds(fringe[0, 0], 1), :]
        down[n:n + 1, :] = fields[c, pl.ds(fringe[0, 1], 1), :]


def start_kernel(state, low_ghost, high_ghost, dmat, out):
    for c, value in homogeneous(state, low_ghost, high_ghost, dmat):
        out[c] = value


def stage_kernel(scale, fringe, rate, state, low_ghost, high_ghost, dmat, out, up, down):
    for c, value in homogeneous(state, low_ghost, high_ghost, dmat):
        out[c] = rate[c] + scale * value
    faces_of(fringe, out, up, down)


def last_kernel(scale, rate, state, low_ghost, high_ghost, dmat, acoustic, out):
    for c, value in homogeneous(state, low_ghost, high_ghost, dmat):
        out[c] = acoustic[c] + STEP * (rate[c] + scale * value)


def unpack_kernel(fringe, payload, weights, rate, out, up, down, rows, codes, source):
    devices, height, coarse = payload.shape
    capacity = (height - CODE_ROWS) // 3
    slots = devices * capacity
    lines = rate.shape[1]
    for c in range(3):
        rows[:, c * coarse:(c + 1) * coarse] = payload[
            :, c * capacity:(c + 1) * capacity, :
        ].reshape(slots, coarse)
    per = 128 // capacity
    tiles = f32(payload[:, 3 * capacity:, :])
    tiles = tiles.reshape(devices // per, per, CODE_ROWS, 128).sum(axis=1)
    for k in range(devices // per):
        codes[:, k * 128:(k + 1) * 128] = jnp.sum(tiles[k], axis=0, keepdims=True).astype(jnp.int32)
    source[...] = jnp.zeros_like(source)

    def one_phase(o, carry):
        combo = lax.broadcasted_iota(jnp.int32, (lines, slots), 0) * PHASES + o
        lands = jnp.where(codes[...] == combo, 1.0, 0.0).astype(jnp.bfloat16)
        gathered = jnp.dot(lands, rows[...], preferred_element_type=jnp.float32)
        gathered = gathered.astype(jnp.bfloat16)
        here = weights[pl.ds(pl.multiple_of(o * coarse, coarse), coarse), :]
        for c in range(3):
            source[c] += jnp.dot(
                gathered[:, c * coarse:(c + 1) * coarse], here, preferred_element_type=jnp.float32
            )
        return carry

    lax.fori_loop(0, PHASES, one_phase, 0)
    out[0] = rate[0]
    for c in range(3):
        out[c + 1] = rate[c + 1] - source[c]
    faces_of(fringe, out, up, down)


def call(kernel, name, inputs, outputs, smem=0, scratch=(), limit=24):
    return pl.pallas_call(
        kernel,
        out_shape=outputs,
        in_specs=[scalars()] * smem + whole(len(inputs) - smem),
        out_specs=jax.tree.map(lambda _: whole(1)[0], outputs),
        scratch_shapes=list(scratch),
        compiler_params=pltpu.CompilerParams(vmem_limit_bytes=limit * MIB),
        name=name,
    )(*inputs)


def exchange(up, down):
    peers = lax.axis_size("ac")
    low = lax.ppermute(up, "ac", [(i, i + 1) for i in range(peers - 1)])
    high = lax.ppermute(down, "ac", [(i + 1, i) for i in range(peers - 1)])
    return low, high


def local(velocity, vorticity, cover, target_line, phase, fringe, acoustic):
    devices = lax.axis_size("les") * lax.axis_size("ac")
    slabs, coarse = velocity.shape[1:]
    lines, cells = acoustic.shape[1:]
    capacity = 2 * slabs * cover.shape[1] // devices
    me = lax.axis_index("les") * lax.axis_size("ac") + lax.axis_index("ac")
    place = (me % (128 // capacity)).reshape(1)

    exact = derivative_matrix(cells)
    high = exact.astype(np.float32).astype(jnp.bfloat16)
    rest = (exact - high.astype(np.float64)).astype(np.float32).astype(jnp.bfloat16)
    dmat = jnp.asarray(np.concatenate([high, rest], axis=1))
    weights = jnp.asarray(lagrange_weights(coarse, cells).astype(jnp.bfloat16))

    state_type = jax.ShapeDtypeStruct(acoustic.shape, jnp.float32)
    face_type = jax.ShapeDtypeStruct((2, cells), jnp.float32)
    staged = (state_type, face_type, face_type)

    def donor(column):
        rows = lax.dynamic_slice_in_dim(acoustic, fringe[0, column], 1, 1)[:, 0]
        return jnp.stack([rows[0], rows[2]])

    ghosts = exchange(donor(0), donor(1))
    payload = pack(
        place, velocity, vorticity, cover.T, target_line.T, phase.T, devices, capacity
    )
    payload = lax.all_to_all(payload, AXES, split_axis=0, concat_axis=0, tiled=True)
    rate = call(start_kernel, "start", (acoustic, *ghosts, dmat), state_type)
    rate, up, down = call(
        unpack_kernel, "unpack", (fringe, payload, weights, rate), staged, smem=1, limit=48,
        scratch=(
            pltpu.VMEM((devices * capacity, 3 * coarse), jnp.bfloat16),
            pltpu.VMEM((1, devices * capacity), jnp.int32),
            pltpu.VMEM((3, lines, cells), jnp.float32),
        ),
    )
    state = rate
    for order in (4, 3):
        low, high = exchange(up, down)
        state, up, down = call(
            functools.partial(stage_kernel, STEP / order), "stage",
            (fringe, rate, state, low, high, dmat), staged, smem=1,
        )
    low, high = exchange(up, down)
    return call(
        functools.partial(last_kernel, STEP / 2), "last",
        (rate, state, low, high, dmat, acoustic), state_type,
    )


def solution(mesh):
    split_rows = P(None, AXES, None)
    pairs = P(AXES, None)
    return jax.shard_map(
        local,
        mesh=mesh,
        in_specs=(split_rows, split_rows, pairs, pairs, pairs, pairs, split_rows),
        out_specs=split_rows,
        check_vma=False,
    )
```

```python
import functools

import jax
import jax.numpy as jnp
import numpy as np
from jax import lax
from jax.experimental import pallas as pl
from jax.experimental.pallas import tpu as pltpu
from jax.sharding import PartitionSpec as P

PHASES = 4
ADVECT = 0.5
STEP = 0.4
AXES = ("les", "ac")
CODE_ROWS = 8
GROUP = 16
PARTS = 4
MIB = 1 << 20
VMEM_LIMIT = 60 * MIB
PAD = 8


def lagrange_weights(coarse, fine):
    table = np.zeros((PHASES, coarse, fine), np.float32)
    for phase in range(PHASES):
        numerator = PHASES * np.arange(fine) + phase
        first_tap = np.clip(numerator // (2 * PHASES) - 1, 0, coarse - 4)
        where_x = numerator.astype(np.float32) / np.float32(2 * PHASES)
        for tap in range(4):
            weight = np.ones((fine,), np.float32)
            for other in range(4):
                if other != tap:
                    gap = where_x - (first_tap + other).astype(np.float32)
                    weight = weight * gap / np.float32(tap - other)
            table[phase, first_tap + tap, np.arange(fine)] += weight
    return table.reshape(PHASES * coarse, fine)


def derivative_matrix(cells):
    off = np.eye(cells, k=1)
    a = np.eye(cells) + 0.25 * (off + off.T)
    b = 0.75 * (off - off.T)
    return np.linalg.solve(a, b).T


def whole(count):
    return [pl.BlockSpec(memory_space=pltpu.VMEM)] * count


def far(count):
    return [pl.BlockSpec(memory_space=pltpu.HBM)] * count


def scalars():
    return pl.BlockSpec(memory_space=pltpu.SMEM)


def f32(x):
    return x.astype(jnp.float32)


def pack_kernel(
    place, velocity, vorticity, cover, line, phase, payload_out,
    payload, table, ranks, vel, vor, cov, lin, pha, arrived, left,
):
    devices = payload.shape[0]
    slabs = vel.shape[1]
    coarse = vel.shape[2]
    capacity = (payload.shape[1] - CODE_ROWS) // 3
    copies = [
        pltpu.make_async_copy(src, dst, arrived.at[n])
        for n, (src, dst) in enumerate(
            ((cover, cov), (line, lin), (phase, pha), (velocity, vel), (vorticity, vor))
        )
    ]
    for copy in copies:
        copy.start()

    copies[0].wait()
    first_block, second_block = cov[0:1, :], cov[1:2, :]
    ids = lax.broadcasted_iota(jnp.int32, (devices, slabs), 0)
    hit = (first_block == ids) | (second_block == ids)
    hit_f = jnp.where(hit, 1.0, 0.0)
    width = 256
    earlier = (
        lax.broadcasted_iota(jnp.int32, (width, width), 0)
        < lax.broadcasted_iota(jnp.int32, (width, width), 1)
    )
    earlier = jnp.where(earlier, 1.0, 0.0).astype(jnp.bfloat16)
    before = jnp.zeros((devices, 1), jnp.float32)
    for k in range(slabs // width):
        part = hit_f[:, k * width:(k + 1) * width]
        rank = jnp.dot(part.astype(jnp.bfloat16), earlier, preferred_element_type=jnp.float32)
        ranks[:, k * width:(k + 1) * width] = jnp.where(part > 0.0, rank + before, -1.0)
        before = before + jnp.sum(part, axis=1, keepdims=True)

    copies[1].wait()
    copies[2].wait()
    code = lin[...] * PHASES + pha[...]
    high = f32((code // 8) * 8)
    low = f32(code % 8)
    row8 = lax.broadcasted_iota(jnp.int32, (128, slabs), 0)
    facts = jnp.where(row8 == 0, high[0:1], 0.0)
    facts = jnp.where(row8 == 1, low[0:1], facts)
    facts = jnp.where(row8 == 2, high[1:2], facts)
    facts = jnp.where(row8 == 3, low[1:2], facts)
    facts = jnp.where(row8 == 4, f32(first_block), facts)
    table[:, 3 * coarse:] = facts.T.astype(jnp.bfloat16)

    copies[3].wait()
    copies[4].wait()
    for c in range(3):
        a, b = (c + 1) % 3, (c + 2) % 3
        lamb = f32(vor[a]) * f32(vel[b]) - f32(vor[b]) * f32(vel[a])
        table[:, c * coarse:(c + 1) * coarse] = lamb.astype(jnp.bfloat16)

    rows16 = lax.broadcasted_iota(jnp.int32, (16, slabs), 0)
    slots = [f32(rows16 + start).astype(jnp.bfloat16) for start in range(0, capacity, 16)]
    one, zero = jnp.bfloat16(1), jnp.bfloat16(0)
    span = GROUP * capacity
    lane_owner = lax.broadcasted_iota(jnp.int32, (1, span), 1) // capacity
    own_lanes = (
        lax.broadcasted_iota(jnp.int32, (GROUP, span), 1) // capacity
        == lax.broadcasted_iota(jnp.int32, (GROUP, span), 0)
    )
    my_part = lax.broadcasted_iota(jnp.int32, (GROUP, 128), 1) // capacity == place[0]
    which_row = lax.broadcasted_iota(jnp.int32, (GROUP, CODE_ROWS, 128), 1)

    def spread(values):
        rows = jnp.where(own_lanes, jnp.broadcast_to(values, (GROUP, span)), 0.0)
        total = rows[:, :128]
        for k in range(1, span // 128):
            total = total + rows[:, k * 128:(k + 1) * 128]
        shift = 64
        while shift >= capacity:
            total = total + pltpu.roll(total, shift, 1)
            shift //= 2
        return jnp.where(my_part, total, 0.0)[:, None, :]

    def group(g, carry):
        first = pl.multiple_of(g * GROUP, GROUP)
        mine = ranks[pl.ds(first, GROUP), :]
        pieces = []
        for n in range(GROUP):
            row = jnp.broadcast_to(mine[n:n + 1, :], (16, slabs)).astype(jnp.bfloat16)
            pieces += [jnp.where(row == slot, one, zero) for slot in slots]
        choose = jnp.concatenate(pieces, axis=0)
        picked = jnp.dot(choose, table[...], preferred_element_type=jnp.float32)
        for c in range(3):
            rows = picked[:, c * coarse:(c + 1) * coarse].reshape(GROUP, capacity, coarse)
            payload[pl.ds(first, GROUP), c * capacity:(c + 1) * capacity, :] = rows.astype(
                jnp.bfloat16
            )
        codes = picked[:, 3 * coarse:].T
        is_first = codes[4:5] == f32(lane_owner + first)
        upper = spread(jnp.where(is_first, codes[0:1], codes[2:3]))
        lower = spread(jnp.where(is_first, codes[1:2], codes[3:4]))
        tile = jnp.where(which_row == 0, upper, jnp.where(which_row == 1, lower, 0.0))
        payload[pl.ds(first, GROUP), 3 * capacity:, :] = tile.astype(jnp.bfloat16)
        leave(g).start()
        return carry

    def leave(g):
        mine = pl.ds(pl.multiple_of(g * GROUP, GROUP), GROUP)
        return pltpu.make_async_copy(payload.at[mine], payload_out.at[mine], left.at[g])

    def gone(g, carry):
        leave(g).wait()
        return carry

    lax.fori_loop(0, devices // GROUP, group, 0)
    lax.fori_loop(0, devices // GROUP, gone, 0)


def pack(place, velocity, vorticity, cover, line, phase, devices, capacity):
    _, slabs, coarse = velocity.shape
    return pl.pallas_call(
        pack_kernel,
        out_shape=jax.ShapeDtypeStruct((devices, 3 * capacity + CODE_ROWS, coarse), jnp.bfloat16),
        in_specs=[scalars()] + far(5),
        out_specs=far(1)[0],
        scratch_shapes=[
            pltpu.VMEM((devices, 3 * capacity + CODE_ROWS, coarse), jnp.bfloat16),
            pltpu.VMEM((slabs, 3 * coarse + 128), jnp.bfloat16),
            pltpu.VMEM((devices, slabs), jnp.float32),
            pltpu.VMEM(velocity.shape, velocity.dtype),
            pltpu.VMEM(vorticity.shape, vorticity.dtype),
            pltpu.VMEM(cover.shape, cover.dtype),
            pltpu.VMEM(line.shape, line.dtype),
            pltpu.VMEM(phase.shape, phase.dtype),
            pltpu.SemaphoreType.DMA((5,)),
            pltpu.SemaphoreType.DMA((devices // GROUP,)),
        ],
        compiler_params=pltpu.CompilerParams(vmem_limit_bytes=VMEM_LIMIT),
        name="pack",
    )(place, velocity, vorticity, cover, line, phase)


def split(x):
    high = x.astype(jnp.bfloat16)
    return high, (x - f32(high)).astype(jnp.bfloat16)


def dx(field, dmat):
    high, low = split(field)
    cells = field.shape[-1]
    both = jnp.dot(high, dmat[...], preferred_element_type=jnp.float32)
    return (
        both[:, :cells]
        + both[:, cells:]
        + jnp.dot(low, dmat[:, :cells], preferred_element_type=jnp.float32)
    )


def dy_inside(field):
    lines = field.shape[0]
    at = lax.broadcasted_iota(jnp.int32, field.shape, 0)
    above = jnp.where(at == lines - 1, 0.0, pltpu.roll(field, lines - 1, 0))
    below = jnp.where(at == 0, 0.0, pltpu.roll(field, 1, 0))
    return (above - below) * 0.5


def homogeneous(state, dmat):
    field = [state[c][...] for c in range(4)]
    dx_p, dx_u = dx(field[0], dmat), dx(field[1], dmat)
    yield 0, -ADVECT * dx_p - dx_u - dy_inside(field[2])
    yield 1, -ADVECT * dx_u - dx_p
    yield 2, -ADVECT * dx(field[2], dmat) - dy_inside(field[0])
    yield 3, -ADVECT * dx(field[3], dmat)


def start_kernel(state, low_ghost, high_ghost, dmat, out):
    lines = state.shape[1]
    for c, value in homogeneous(state, dmat):
        out[c] = value
    for c, n in ((0, 1), (2, 0)):
        out[c, 0:1, :] += 0.5 * low_ghost[n:n + 1]
        out[c, lines - 1:lines, :] -= 0.5 * high_ghost[n:n + 1]


def inside_kernel(rate, dmat, acoustic, out, one, two):
    for c, value in homogeneous(rate, dmat):
        one[c] = rate[c] + FIRST * value
    for c, value in homogeneous(one, dmat):
        two[c] = rate[c] + SECOND * value
    for c, value in homogeneous(two, dmat):
        out[c] = acoustic[c] + STEP * (rate[c] + THIRD * value)


FIRST, SECOND, THIRD = STEP / 4, STEP / 3, STEP / 2


def edge_kernel(lines, peers, here_at, got, dmat, inside, out, fix):
    me = here_at[0]

    def bundle(by):
        exists = (me + by >= 0) & (me + by < peers)
        return jnp.where(exists, got[jnp.clip(me + by, 0, peers - 1)], 0.0)

    def pair(sent, level, column):
        first = 4 * level + 2 * column
        return sent[first:first + 1, :], sent[first + 1:first + 2, :]

    def at(sent, column, line):
        return sent[12 + column:13 + column, :] == float(line + 1)

    def first_change(sign, ghost):
        p, v = ghost
        return 0.5 * sign * FIRST * v, 0.5 * sign * FIRST * p

    def second_level(sent, column, low, high):
        p, v = pair(sent, 1, column)
        for sign, line, ghost in ((1, 0, low), (-1, lines - 1, high)):
            dp, dv = first_change(sign, ghost)
            here = at(sent, column, line)
            p, v = p + jnp.where(here, dp, 0.0), v + jnp.where(here, dv, 0.0)
        return p, v

    @pl.when(pl.program_id(0) == 0)
    def _():
        mine, back1, back2, back3 = (bundle(-n) for n in range(4))
        next1, next2, next3 = (bundle(n) for n in range(1, 4))
        up0, up1, up2 = pair(mine, 0, 0), pair(back1, 0, 0), pair(back2, 0, 0)
        down0, down1, down2 = pair(mine, 0, 1), pair(next1, 0, 1), pair(next2, 0, 1)
        up3, down3 = pair(back3, 0, 0), pair(next3, 0, 1)
        second_up = [
            second_level(mine, 0, up1, down1),
            second_level(back1, 0, up2, down0),
            second_level(back2, 0, up3, pair(back1, 0, 1)),
        ]
        second_down = [
            second_level(mine, 1, up1, down1),
            second_level(next1, 1, up0, down2),
            second_level(next2, 1, pair(next1, 0, 0), down3),
        ]
        ends = [
            (1, up1, second_up[1]), (-1, down1, second_down[1]),
            (1, up2, second_up[2]), (-1, down0, second_down[0]),
            (1, up0, second_up[0]), (-1, down2, second_down[2]),
        ]
        changes = [first_change(sign, ghost) for sign, ghost, _ in ends]
        slopes = dx(jnp.concatenate([x for pv in changes for x in pv] + [jnp.zeros_like(up0[0])] * 4), dmat)
        seconds = []
        for n, (sign, _, ghost) in enumerate(ends):
            dp, dv = changes[n]
            sp, sv = slopes[2 * n:2 * n + 1], slopes[2 * n + 1:2 * n + 2]
            edge = (
                SECOND * (-ADVECT * sp + 0.5 * sign * ghost[1]),
                SECOND * -sp,
                SECOND * (-ADVECT * sv + 0.5 * sign * ghost[0]),
            )
            seconds.append((edge, (0.5 * SECOND * sign * dv, 0.5 * SECOND * sign * dp)))

        def third_level(sent, column, low, high):
            p, v = pair(sent, 2, column)
            for line, step, (edge, inner) in ((0, 1, low), (lines - 1, -1, high)):
                for where, dp, dv in ((line, edge[0], edge[2]), (line + step, *inner)):
                    here = at(sent, column, where)
                    p, v = p + jnp.where(here, dp, 0.0), v + jnp.where(here, dv, 0.0)
            return p, v

        ghosts = (
            third_level(back1, 0, seconds[2], seconds[3]),
            third_level(next1, 1, seconds[4], seconds[5]),
        )
        rows = [x for edge, inner in seconds[:2] for x in (*edge, *inner)]
        slopes = dx(jnp.concatenate(rows + [jnp.zeros_like(rows[0])] * 6), dmat)
        for n, sign in enumerate((1, -1)):
            (p0, u0, v0), (p1, v1) = seconds[n]
            sp0, su0, sv0, sp1, sv1 = (slopes[5 * n + k:5 * n + k + 1] for k in range(5))
            half = 0.5 * sign
            ghost_p, ghost_v = ghosts[n]
            change = (
                (-ADVECT * sp0 - su0 - half * v1 + half * ghost_v, -ADVECT * sp1 + half * v0, half * v1),
                (-ADVECT * su0 - sp0, -sp1, jnp.zeros_like(p0)),
                (-ADVECT * sv0 - half * p1 + half * ghost_p, -ADVECT * sv1 + half * p0, half * p1),
            )
            fix[n] = jnp.zeros(fix.shape[1:], fix.dtype)
            for c in range(3):
                for k in range(3):
                    row = k if n == 0 else 7 - k
                    fix[n, c, row:row + 1, :] = STEP * THIRD * change[c][k]

    out[...] = inside[...] + fix[pl.program_id(0)]


def add_edges(inside, dmat, got, here_at):
    fields, lines, cells = inside.shape
    block = pl.BlockSpec((fields, 8, cells), lambda i: (0, i * (lines // 8 - 1), 0))
    return pl.pallas_call(
        functools.partial(edge_kernel, lines, got.shape[0]),
        out_shape=jax.ShapeDtypeStruct(inside.shape, inside.dtype),
        grid=(2,),
        in_specs=[scalars()] + whole(2) + [block],
        out_specs=block,
        scratch_shapes=[pltpu.VMEM((2, fields, 8, cells), jnp.float32)],
        input_output_aliases={3: 0},
        compiler_params=pltpu.CompilerParams(vmem_limit_bytes=VMEM_LIMIT),
        name="edges",
    )(here_at, got, dmat, inside)


def receive_kernel(
    fringe, payload, weights_in, rate_in, dmat_in, out, sent,
    held, lands, rows, total, weights, rate, dmat, state, bundle, arrived, left,
):
    devices, height, coarse = payload.shape
    capacity = (height - CODE_ROWS) // 3
    lines = rate.shape[1]
    cells = rate.shape[2]
    part = devices // PARTS
    copies = [
        pltpu.make_async_copy(
            payload.at[k * part:(k + 1) * part], held.at[k * part:(k + 1) * part], arrived.at[k]
        )
        for k in range(PARTS)
    ]
    others = [
        pltpu.make_async_copy(src, dst, arrived.at[PARTS + k])
        for k, (src, dst) in enumerate(((weights_in, weights), (rate_in, rate), (dmat_in, dmat)))
    ]
    for copy in copies + others:
        copy.start()
    per = 128 // capacity
    tiles = part // per
    slots = part * capacity
    one, zero = jnp.bfloat16(1), jnp.bfloat16(0)
    row16 = lax.broadcasted_iota(jnp.int32, (16, slots), 0)
    for k, copy in enumerate(copies):
        copy.wait()
        mine = held.at[k * part:(k + 1) * part]
        codes = f32(mine[:, 3 * capacity:, :])
        codes = codes.reshape(tiles, per, CODE_ROWS, 128).sum(axis=1)
        codes = codes.sum(axis=1).astype(jnp.int32)
        phases = f32(codes % PHASES)
        phases = jnp.concatenate([phases, jnp.zeros((128 - tiles, 128), jnp.float32)], axis=0).T
        target = f32(codes // PHASES - lines // 2)
        target = jnp.concatenate([target[n:n + 1, :] for n in range(tiles)], axis=1)
        target = jnp.broadcast_to(target, (16, slots)).astype(jnp.bfloat16)
        for n in range(lines // 16):
            line = f32(row16 + (16 * n - lines // 2)).astype(jnp.bfloat16)
            lands[16 * n:16 * (n + 1), :] = jnp.where(target == line, one, zero)
        for n in range(tiles):
            phase = jnp.broadcast_to(phases[:, n:n + 1], (128, coarse)).astype(jnp.bfloat16)
            for c in range(3):
                values = mine[n * per:(n + 1) * per, c * capacity:(c + 1) * capacity, :]
                values = values.reshape(128, coarse)
                for o in range(PHASES):
                    at = (c * PHASES + o) * coarse
                    rows[128 * n:128 * (n + 1), at:at + coarse] = jnp.where(
                        phase == jnp.bfloat16(o), values, zero
                    )
        landed = jnp.dot(lands[...], rows[...], preferred_element_type=jnp.float32)
        total[...] = landed if k == 0 else total[...] + landed
    for copy in others:
        copy.wait()
    inner = slice(PAD, PAD + lines)
    state[:, :PAD, :] = jnp.zeros((4, PAD, cells), jnp.float32)
    state[:, PAD + lines:, :] = jnp.zeros((4, PAD, cells), jnp.float32)
    state[0, inner, :] = rate[0]
    deep = PHASES * coarse
    for c in range(3):
        gathered = total[:, c * deep:(c + 1) * deep].astype(jnp.bfloat16)
        source = jnp.dot(gathered, weights[...], preferred_element_type=jnp.float32)
        state[c + 1, inner, :] = rate[c + 1] - source
    leave = pltpu.make_async_copy(state.at[:, inner, :], out, left.at[0])
    leave.start()

    blank = jnp.zeros((1, cells), jnp.float32)
    near = [
        [[state[c, pl.ds(PAD + fringe[0, n] + k, 1), :] for k in range(-2, 3)] for c in range(3)]
        for n in range(2)
    ]
    slopes = [near[n][c][k] for n in range(2) for c in range(3) for k in (1, 2, 3)]
    slopes = dx(jnp.concatenate(slopes + [blank] * 6, axis=0), dmat)
    stage = []
    for n in range(2):
        p, u, v = near[n]
        dp, du, dv = (
            [slopes[9 * n + 3 * c + k:9 * n + 3 * c + k + 1] for k in range(3)] for c in range(3)
        )
        stage.append([[], [], []])
        for k in range(3):
            line = fringe[0, n] + k - 1
            real = (line >= 0) & (line < lines)
            change = (
                -ADVECT * dp[k] - du[k] - 0.5 * (v[k + 2] - v[k]),
                -ADVECT * du[k] - dp[k],
                -ADVECT * dv[k] - 0.5 * (p[k + 2] - p[k]),
            )
            for c in range(3):
                value = near[n][c][k + 1] + FIRST * change[c]
                stage[n][c].append(jnp.where(real, value, 0.0))
    slopes = [stage[n][c][1] for n in range(2) for c in range(3)]
    slopes = dx(jnp.concatenate(slopes + [blank] * 2, axis=0), dmat)
    for n in range(2):
        p, _, v = stage[n]
        dp, du, dv = (slopes[3 * n + c:3 * n + c + 1] for c in range(3))
        last_p = near[n][0][2] + SECOND * (-ADVECT * dp - du - 0.5 * (v[2] - v[0]))
        last_v = near[n][2][2] + SECOND * (-ADVECT * dv - 0.5 * (p[2] - p[0]))
        for level, pair in enumerate(((near[n][0][2], near[n][2][2]), (p[1], v[1]), (last_p, last_v))):
            for k in range(2):
                at = 4 * level + 2 * n + k
                bundle[at:at + 1, :] = pair[k]
        bundle[12 + n:13 + n, :] = jnp.full((1, cells), (fringe[0, n] + 1).astype(jnp.float32))
        bundle[14 + n:15 + n, :] = blank
    sent[...] = jnp.broadcast_to(bundle[...][None], sent.shape)
    leave.wait()


def call(kernel, name, inputs, outputs, smem=0):
    return pl.pallas_call(
        kernel,
        out_shape=outputs,
        in_specs=[scalars()] * smem + whole(len(inputs) - smem),
        out_specs=jax.tree.map(lambda _: whole(1)[0], outputs),
        compiler_params=pltpu.CompilerParams(vmem_limit_bytes=VMEM_LIMIT),
        name=name,
    )(*inputs)


def shifted(x, by):
    peers = lax.axis_size("ac")
    pairs = [(i, i + by) for i in range(peers) if 0 <= i + by < peers]
    return lax.ppermute(x, "ac", pairs)


def local(velocity, vorticity, cover, target_line, phase, fringe, acoustic):
    devices = lax.axis_size("les") * lax.axis_size("ac")
    slabs, coarse = velocity.shape[1:]
    lines, cells = acoustic.shape[1:]
    capacity = 2 * slabs * cover.shape[1] // devices
    me = lax.axis_index("les") * lax.axis_size("ac") + lax.axis_index("ac")
    place = (me % (128 // capacity)).reshape(1)

    exact = derivative_matrix(cells)
    high = exact.astype(np.float32).astype(jnp.bfloat16)
    rest = (exact - high.astype(np.float64)).astype(np.float32).astype(jnp.bfloat16)
    dmat = jnp.asarray(np.concatenate([high, rest], axis=1))
    weights = jnp.asarray(lagrange_weights(coarse, cells).astype(jnp.bfloat16))

    state_type = jax.ShapeDtypeStruct(acoustic.shape, jnp.float32)

    def donor(column):
        rows = lax.dynamic_slice_in_dim(acoustic, fringe[0, column], 1, 1)[:, 0]
        return jnp.stack([rows[0], rows[2]])

    ghosts = (shifted(donor(0), 1), shifted(donor(1), -1))
    payload = pack(
        place, velocity, vorticity, cover.T, target_line.T, phase.T, devices, capacity
    )
    payload = lax.all_to_all(payload, AXES, split_axis=0, concat_axis=0, tiled=True)
    rate = call(start_kernel, "start", (acoustic, *ghosts, dmat), state_type)
    peers = lax.axis_size("ac")
    part = devices // PARTS * capacity
    rate, sent = pl.pallas_call(
        receive_kernel,
        out_shape=(state_type, jax.ShapeDtypeStruct((peers, 16, cells), jnp.float32)),
        in_specs=[scalars()] + far(4),
        out_specs=(far(1)[0], whole(1)[0]),
        scratch_shapes=[
            pltpu.VMEM(payload.shape, payload.dtype),
            pltpu.VMEM((lines, part), jnp.bfloat16),
            pltpu.VMEM((part, 3 * PHASES * coarse), jnp.bfloat16),
            pltpu.VMEM((lines, 3 * PHASES * coarse), jnp.float32),
            pltpu.VMEM(weights.shape, weights.dtype),
            pltpu.VMEM(acoustic.shape, jnp.float32),
            pltpu.VMEM(dmat.shape, dmat.dtype),
            pltpu.VMEM((4, lines + 2 * PAD, cells), jnp.float32),
            pltpu.VMEM((16, cells), jnp.float32),
            pltpu.SemaphoreType.DMA((PARTS + 3,)),
            pltpu.SemaphoreType.DMA((1,)),
        ],
        compiler_params=pltpu.CompilerParams(vmem_limit_bytes=VMEM_LIMIT),
        name="receive",
    )(fringe, payload, weights, rate, dmat)
    got = lax.all_to_all(sent, "ac", split_axis=0, concat_axis=0, tiled=True)
    inside = pl.pallas_call(
        inside_kernel,
        out_shape=state_type,
        in_specs=whole(3),
        out_specs=whole(1)[0],
        scratch_shapes=[pltpu.VMEM(acoustic.shape, jnp.float32)] * 2,
        compiler_params=pltpu.CompilerParams(vmem_limit_bytes=VMEM_LIMIT),
        name="inside",
    )(rate, dmat, acoustic)
    return add_edges(inside, dmat, got, lax.axis_index("ac").reshape(1))


def solution(mesh):
    split_rows = P(None, AXES, None)
    pairs = P(AXES, None)
    return jax.shard_map(
        local,
        mesh=mesh,
        in_specs=(split_rows, split_rows, pairs, pairs, pairs, pairs, split_rows),
        out_specs=split_rows,
        check_vma=False,
    )
```

```python
import functools

import jax
import jax.numpy as jnp
import numpy as np
from jax import lax
from jax.experimental import pallas as pl
from jax.experimental.pallas import tpu as pltpu
from jax.sharding import PartitionSpec as P

PHASES = 4
ADVECT = 0.5
STEP = 0.4
AXES = ("les", "ac")
CODE_ROWS = 8
GROUP = 16
PARTS = 2
MIB = 1 << 20
VMEM_LIMIT = 60 * MIB
DONORS_LIMIT = 60 * MIB
EDGES_LIMIT = 32 * MIB
WINDOW = 5


def lagrange_weights(coarse, fine):
    table = np.zeros((PHASES, coarse, fine), np.float32)
    for phase in range(PHASES):
        numerator = PHASES * np.arange(fine) + phase
        first_tap = np.clip(numerator // (2 * PHASES) - 1, 0, coarse - 4)
        where_x = numerator.astype(np.float32) / np.float32(2 * PHASES)
        for tap in range(4):
            weight = np.ones((fine,), np.float32)
            for other in range(4):
                if other != tap:
                    gap = where_x - (first_tap + other).astype(np.float32)
                    weight = weight * gap / np.float32(tap - other)
            table[phase, first_tap + tap, np.arange(fine)] += weight
    return table.reshape(PHASES * coarse, fine)


def derivative_matrix(cells):
    off = np.eye(cells, k=1)
    a = np.eye(cells) + 0.25 * (off + off.T)
    b = 0.75 * (off - off.T)
    return np.linalg.solve(a, b).T


def whole(count):
    return [pl.BlockSpec(memory_space=pltpu.VMEM)] * count


def far(count):
    return [pl.BlockSpec(memory_space=pltpu.HBM)] * count


def scalars():
    return pl.BlockSpec(memory_space=pltpu.SMEM)


def f32(x):
    return x.astype(jnp.float32)


def pack_kernel(
    place, velocity, vorticity, cover, line, phase, payload_out,
    payload, table, ranks, vel, vor, cov, lin, pha, arrived, left,
):
    devices = payload.shape[0]
    slabs = vel.shape[1]
    coarse = vel.shape[2]
    capacity = (payload.shape[1] - CODE_ROWS) // 3
    copies = [
        pltpu.make_async_copy(src, dst, arrived.at[n])
        for n, (src, dst) in enumerate(
            ((cover, cov), (line, lin), (phase, pha), (velocity, vel), (vorticity, vor))
        )
    ]
    for copy in copies:
        copy.start()

    copies[0].wait()
    first_block, second_block = cov[0:1, :], cov[1:2, :]
    ids = lax.broadcasted_iota(jnp.int32, (devices, slabs), 0)
    hit = (first_block == ids) | (second_block == ids)
    hit_f = jnp.where(hit, 1.0, 0.0)
    width = 256
    earlier = (
        lax.broadcasted_iota(jnp.int32, (width, width), 0)
        < lax.broadcasted_iota(jnp.int32, (width, width), 1)
    )
    earlier = jnp.where(earlier, 1.0, 0.0).astype(jnp.bfloat16)
    before = jnp.zeros((devices, 1), jnp.float32)
    for k in range(slabs // width):
        part = hit_f[:, k * width:(k + 1) * width]
        rank = jnp.dot(part.astype(jnp.bfloat16), earlier, preferred_element_type=jnp.float32)
        ranks[:, k * width:(k + 1) * width] = jnp.where(part > 0.0, rank + before, -1.0)
        before = before + jnp.sum(part, axis=1, keepdims=True)

    copies[1].wait()
    copies[2].wait()
    code = lin[...] * PHASES + pha[...]
    high = f32((code // 8) * 8)
    low = f32(code % 8)
    row8 = lax.broadcasted_iota(jnp.int32, (128, slabs), 0)
    facts = jnp.where(row8 == 0, high[0:1], 0.0)
    facts = jnp.where(row8 == 1, low[0:1], facts)
    facts = jnp.where(row8 == 2, high[1:2], facts)
    facts = jnp.where(row8 == 3, low[1:2], facts)
    facts = jnp.where(row8 == 4, f32(first_block), facts)
    table[:, 3 * coarse:] = facts.T.astype(jnp.bfloat16)

    copies[3].wait()
    copies[4].wait()
    for c in range(3):
        a, b = (c + 1) % 3, (c + 2) % 3
        lamb = f32(vor[a]) * f32(vel[b]) - f32(vor[b]) * f32(vel[a])
        table[:, c * coarse:(c + 1) * coarse] = lamb.astype(jnp.bfloat16)

    rows16 = lax.broadcasted_iota(jnp.int32, (16, slabs), 0)
    slots = [f32(rows16 + start).astype(jnp.bfloat16) for start in range(0, capacity, 16)]
    one, zero = jnp.bfloat16(1), jnp.bfloat16(0)
    span = GROUP * capacity
    lane_owner = lax.broadcasted_iota(jnp.int32, (1, span), 1) // capacity
    own_lanes = (
        lax.broadcasted_iota(jnp.int32, (GROUP, span), 1) // capacity
        == lax.broadcasted_iota(jnp.int32, (GROUP, span), 0)
    )
    my_part = lax.broadcasted_iota(jnp.int32, (GROUP, 128), 1) // capacity == place[0]
    which_row = lax.broadcasted_iota(jnp.int32, (GROUP, CODE_ROWS, 128), 1)

    def spread(values):
        rows = jnp.where(own_lanes, jnp.broadcast_to(values, (GROUP, span)), 0.0)
        total = rows[:, :128]
        for k in range(1, span // 128):
            total = total + rows[:, k * 128:(k + 1) * 128]
        shift = 64
        while shift >= capacity:
            total = total + pltpu.roll(total, shift, 1)
            shift //= 2
        return jnp.where(my_part, total, 0.0)[:, None, :]

    def group(g, carry):
        first = pl.multiple_of(g * GROUP, GROUP)
        mine = ranks[pl.ds(first, GROUP), :]
        pieces = []
        for n in range(GROUP):
            row = jnp.broadcast_to(mine[n:n + 1, :], (16, slabs)).astype(jnp.bfloat16)
            pieces += [jnp.where(row == slot, one, zero) for slot in slots]
        choose = jnp.concatenate(pieces, axis=0)
        picked = jnp.dot(choose, table[...], preferred_element_type=jnp.float32)
        for c in range(3):
            rows = picked[:, c * coarse:(c + 1) * coarse].reshape(GROUP, capacity, coarse)
            payload[pl.ds(first, GROUP), c * capacity:(c + 1) * capacity, :] = rows.astype(
                jnp.bfloat16
            )
        codes = picked[:, 3 * coarse:].T
        is_first = codes[4:5] == f32(lane_owner + first)
        upper = spread(jnp.where(is_first, codes[0:1], codes[2:3]))
        lower = spread(jnp.where(is_first, codes[1:2], codes[3:4]))
        tile = jnp.where(which_row == 0, upper, jnp.where(which_row == 1, lower, 0.0))
        payload[pl.ds(first, GROUP), 3 * capacity:, :] = tile.astype(jnp.bfloat16)
        leave(g).start()
        return carry

    def leave(g):
        mine = pl.ds(pl.multiple_of(g * GROUP, GROUP), GROUP)
        return pltpu.make_async_copy(payload.at[mine], payload_out.at[mine], left.at[g])

    def gone(g, carry):
        leave(g).wait()
        return carry

    lax.fori_loop(0, devices // GROUP, group, 0, unroll=True)
    lax.fori_loop(0, devices // GROUP, gone, 0)


def pack(place, velocity, vorticity, cover, line, phase, devices, capacity):
    _, slabs, coarse = velocity.shape
    return pl.pallas_call(
        pack_kernel,
        out_shape=jax.ShapeDtypeStruct((devices, 3 * capacity + CODE_ROWS, coarse), jnp.bfloat16),
        in_specs=[scalars()] + far(5),
        out_specs=far(1)[0],
        scratch_shapes=[
            pltpu.VMEM((devices, 3 * capacity + CODE_ROWS, coarse), jnp.bfloat16),
            pltpu.VMEM((slabs, 3 * coarse + 128), jnp.bfloat16),
            pltpu.VMEM((devices, slabs), jnp.float32),
            pltpu.VMEM(velocity.shape, velocity.dtype),
            pltpu.VMEM(vorticity.shape, vorticity.dtype),
            pltpu.VMEM(cover.shape, cover.dtype),
            pltpu.VMEM(line.shape, line.dtype),
            pltpu.VMEM(phase.shape, phase.dtype),
            pltpu.SemaphoreType.DMA((5,)),
            pltpu.SemaphoreType.DMA((devices // GROUP,)),
        ],
        compiler_params=pltpu.CompilerParams(vmem_limit_bytes=VMEM_LIMIT),
        name="pack",
    )(place, velocity, vorticity, cover, line, phase)


def split(x):
    high = x.astype(jnp.bfloat16)
    return high, (x - f32(high)).astype(jnp.bfloat16)


def dx(field, dmat):
    high, low = split(field)
    cells = field.shape[-1]
    both = jnp.dot(high, dmat[...], preferred_element_type=jnp.float32)
    return (
        both[:, :cells]
        + both[:, cells:]
        + jnp.dot(low, dmat[:, :cells], preferred_element_type=jnp.float32)
    )


def dx_rounded(field, dmat):
    return jnp.dot(
        field.astype(jnp.bfloat16), dmat[:, :field.shape[-1]], preferred_element_type=jnp.float32
    )


def dy_inside(field):
    lines = field.shape[0]
    at = lax.broadcasted_iota(jnp.int32, field.shape, 0)
    above = jnp.where(at == lines - 1, 0.0, pltpu.roll(field, lines - 1, 0))
    below = jnp.where(at == 0, 0.0, pltpu.roll(field, 1, 0))
    return (above - below) * 0.5


def homogeneous(state, dmat, dx=dx):
    field = [state[c][...] for c in range(4)]
    dx_p, dx_u = dx(field[0], dmat), dx(field[1], dmat)
    yield 0, -ADVECT * dx_p - dx_u - dy_inside(field[2])
    yield 1, -ADVECT * dx_u - dx_p
    yield 2, -ADVECT * dx(field[2], dmat) - dy_inside(field[0])
    yield 3, -ADVECT * dx(field[3], dmat)


def start_kernel(fringe, state, low_ghost, high_ghost, dmat, out, near):
    lines, cells = state.shape[1:]
    for c, value in homogeneous(state, dmat):
        out[c] = value
    for c, n in ((0, 1), (2, 0)):
        out[c, 0:1, :] += 0.5 * low_ghost[n:n + 1]
        out[c, lines - 1:lines, :] -= 0.5 * high_ghost[n:n + 1]
    near[...] = jnp.zeros_like(near)
    for n in range(2):
        for c in range(3):
            for k in range(WINDOW):
                line = fringe[0, n] + (k - 2)
                row = out[c, pl.ds(jnp.clip(line, 0, lines - 1), 1), :]
                at = (n * 3 + c) * 8 + k
                near[at:at + 1, :] = jnp.where((line >= 0) & (line < lines), row, 0.0)


FIRST, SECOND, THIRD = STEP / 4, STEP / 3, STEP / 2


def edge_kernel(lines, peers, here_at, got, dmat, inside, out, fix):
    me = here_at[0]

    def bundle(by):
        exists = (me + by >= 0) & (me + by < peers)
        return jnp.where(exists, got[jnp.clip(me + by, 0, peers - 1)], 0.0)

    def pair(sent, level, column):
        first = 4 * level + 2 * column
        return sent[first:first + 1, :], sent[first + 1:first + 2, :]

    def at(sent, column, line):
        return sent[12 + column:13 + column, :] == float(line + 1)

    def first_change(sign, ghost):
        p, v = ghost
        return 0.5 * sign * FIRST * v, 0.5 * sign * FIRST * p

    def second_level(sent, column, low, high):
        p, v = pair(sent, 1, column)
        for sign, line, ghost in ((1, 0, low), (-1, lines - 1, high)):
            dp, dv = first_change(sign, ghost)
            here = at(sent, column, line)
            p, v = p + jnp.where(here, dp, 0.0), v + jnp.where(here, dv, 0.0)
        return p, v

    @pl.when(pl.program_id(0) == 0)
    def _():
        mine, back1, back2, back3 = (bundle(-n) for n in range(4))
        next1, next2, next3 = (bundle(n) for n in range(1, 4))
        up0, up1, up2 = pair(mine, 0, 0), pair(back1, 0, 0), pair(back2, 0, 0)
        down0, down1, down2 = pair(mine, 0, 1), pair(next1, 0, 1), pair(next2, 0, 1)
        up3, down3 = pair(back3, 0, 0), pair(next3, 0, 1)
        second_up = [
            second_level(mine, 0, up1, down1),
            second_level(back1, 0, up2, down0),
            second_level(back2, 0, up3, pair(back1, 0, 1)),
        ]
        second_down = [
            second_level(mine, 1, up1, down1),
            second_level(next1, 1, up0, down2),
            second_level(next2, 1, pair(next1, 0, 0), down3),
        ]
        ends = [
            (1, up1, second_up[1]), (-1, down1, second_down[1]),
            (1, up2, second_up[2]), (-1, down0, second_down[0]),
            (1, up0, second_up[0]), (-1, down2, second_down[2]),
        ]
        changes = [first_change(sign, ghost) for sign, ghost, _ in ends]
        slopes = dx(jnp.concatenate([x for pv in changes for x in pv] + [jnp.zeros_like(up0[0])] * 4), dmat)
        seconds = []
        for n, (sign, _, ghost) in enumerate(ends):
            dp, dv = changes[n]
            sp, sv = slopes[2 * n:2 * n + 1], slopes[2 * n + 1:2 * n + 2]
            edge = (
                SECOND * (-ADVECT * sp + 0.5 * sign * ghost[1]),
                SECOND * -sp,
                SECOND * (-ADVECT * sv + 0.5 * sign * ghost[0]),
            )
            seconds.append((edge, (0.5 * SECOND * sign * dv, 0.5 * SECOND * sign * dp)))

        def third_level(sent, column, low, high):
            p, v = pair(sent, 2, column)
            for line, step, (edge, inner) in ((0, 1, low), (lines - 1, -1, high)):
                for where, dp, dv in ((line, edge[0], edge[2]), (line + step, *inner)):
                    here = at(sent, column, where)
                    p, v = p + jnp.where(here, dp, 0.0), v + jnp.where(here, dv, 0.0)
            return p, v

        ghosts = (
            third_level(back1, 0, seconds[2], seconds[3]),
            third_level(next1, 1, seconds[4], seconds[5]),
        )
        rows = [x for edge, inner in seconds[:2] for x in (*edge, *inner)]
        slopes = dx(jnp.concatenate(rows + [jnp.zeros_like(rows[0])] * 6), dmat)
        for n, sign in enumerate((1, -1)):
            (p0, u0, v0), (p1, v1) = seconds[n]
            sp0, su0, sv0, sp1, sv1 = (slopes[5 * n + k:5 * n + k + 1] for k in range(5))
            half = 0.5 * sign
            ghost_p, ghost_v = ghosts[n]
            change = (
                (-ADVECT * sp0 - su0 - half * v1 + half * ghost_v, -ADVECT * sp1 + half * v0, half * v1),
                (-ADVECT * su0 - sp0, -sp1, jnp.zeros_like(p0)),
                (-ADVECT * sv0 - half * p1 + half * ghost_p, -ADVECT * sv1 + half * p0, half * p1),
            )
            fix[n] = jnp.zeros(fix.shape[1:], fix.dtype)
            for c in range(3):
                for k in range(3):
                    row = k if n == 0 else 7 - k
                    fix[n, c, row:row + 1, :] = STEP * THIRD * change[c][k]

    out[...] = inside[...] + fix[pl.program_id(0)]


def add_edges(inside, dmat, got, here_at):
    fields, lines, cells = inside.shape
    block = pl.BlockSpec((fields, 8, cells), lambda i: (0, i * (lines // 8 - 1), 0))
    return pl.pallas_call(
        functools.partial(edge_kernel, lines, got.shape[0]),
        out_shape=jax.ShapeDtypeStruct(inside.shape, inside.dtype),
        grid=(2,),
        in_specs=[scalars()] + whole(2) + [block],
        out_specs=block,
        scratch_shapes=[pltpu.VMEM((2, fields, 8, cells), jnp.float32)],
        input_output_aliases={3: 0},
        compiler_params=pltpu.CompilerParams(vmem_limit_bytes=EDGES_LIMIT),
        name="edges",
    )(here_at, got, dmat, inside)


def codes_of(payload, capacity):
    per = 128 // capacity
    codes = f32(payload[:, 3 * capacity:, :])
    codes = codes.reshape(payload.shape[0] // per, per, CODE_ROWS, 128).sum(axis=1)
    return codes.sum(axis=1)


def in_one_row(values):
    return jnp.concatenate([values[n:n + 1, :] for n in range(values.shape[0])], axis=1)


def donors_kernel(
    lines, fringe, payload, weights_in, near_in, dmat_in, sent,
    rows, bundle, weights, near_rows, dmat, arrived,
):
    copies = [
        pltpu.make_async_copy(src, dst, arrived.at[k])
        for k, (src, dst) in enumerate(
            ((weights_in, weights), (near_in, near_rows), (dmat_in, dmat))
        )
    ]
    for copy in copies:
        copy.start()
    devices, height, coarse = payload.shape
    capacity = (height - CODE_ROWS) // 3
    slots = devices * capacity
    cells = weights.shape[1]
    codes = in_one_row(codes_of(payload, capacity))
    for c in range(2):
        rows[:, c * coarse:(c + 1) * coarse] = payload[
            :, c * capacity:(c + 1) * capacity, :
        ].reshape(slots, coarse)
    for copy in copies:
        copy.wait()
    side = 24
    at = lax.broadcasted_iota(jnp.int32, (2 * side, 1), 0)
    base = jnp.where(at < side, fringe[0, 0], fringe[0, 1])
    combo = f32((base - 2) * PHASES + at % side)
    lands = jnp.where(codes == combo, 1.0, 0.0).astype(jnp.bfloat16)
    gathered = jnp.dot(lands, rows[...], preferred_element_type=jnp.float32)
    source = jnp.zeros((4 * side, cells), jnp.float32)
    both = jnp.concatenate([gathered[:, :coarse], gathered[:, coarse:]], axis=0)
    phase = lax.broadcasted_iota(jnp.int32, both.shape, 0) % PHASES
    for o in range(PHASES):
        chosen = jnp.where(phase == o, both, 0.0).astype(jnp.bfloat16)
        source += jnp.dot(
            chosen, weights[o * coarse:(o + 1) * coarse, :], preferred_element_type=jnp.float32
        )
    source = source.reshape(4 * side // PHASES, PHASES, cells).sum(axis=1)

    def rate_row(n, c, k):
        first = (n * 3 + c) * 8 + k
        row = near_rows[first:first + 1, :]
        if c > 0:
            first = (c - 1) * 2 * side // PHASES + n * side // PHASES + k
            row = row - source[first:first + 1]
        return row

    blank = jnp.zeros((1, cells), jnp.float32)
    near = [[[rate_row(n, c, k) for k in range(WINDOW)] for c in range(3)] for n in range(2)]
    slopes = [near[n][c][k] for n in range(2) for c in range(3) for k in (1, 2, 3)]
    slopes = dx(jnp.concatenate(slopes + [blank] * 6, axis=0), dmat)
    stage = []
    for n in range(2):
        p, u, v = near[n]
        dp, du, dv = (
            [slopes[9 * n + 3 * c + k:9 * n + 3 * c + k + 1] for k in range(3)] for c in range(3)
        )
        stage.append([[], [], []])
        for k in range(3):
            line = fringe[0, n] + k - 1
            real = (line >= 0) & (line < lines)
            change = (
                -ADVECT * dp[k] - du[k] - 0.5 * (v[k + 2] - v[k]),
                -ADVECT * du[k] - dp[k],
                -ADVECT * dv[k] - 0.5 * (p[k + 2] - p[k]),
            )
            for c in range(3):
                value = near[n][c][k + 1] + FIRST * change[c]
                stage[n][c].append(jnp.where(real, value, 0.0))
    slopes = [stage[n][c][1] for n in range(2) for c in range(3)]
    slopes = dx(jnp.concatenate(slopes + [blank] * 2, axis=0), dmat)
    for n in range(2):
        p, _, v = stage[n]
        dp, du, dv = (slopes[3 * n + c:3 * n + c + 1] for c in range(3))
        last_p = near[n][0][2] + SECOND * (-ADVECT * dp - du - 0.5 * (v[2] - v[0]))
        last_v = near[n][2][2] + SECOND * (-ADVECT * dv - 0.5 * (p[2] - p[0]))
        levels = (near[n][0][2], near[n][2][2]), (p[1], v[1]), (last_p, last_v)
        for level, pair in enumerate(levels):
            for k in range(2):
                at = 4 * level + 2 * n + k
                bundle[at:at + 1, :] = pair[k]
        bundle[12 + n:13 + n, :] = jnp.full((1, cells), (fringe[0, n] + 1).astype(jnp.float32))
        bundle[14 + n:15 + n, :] = blank
    sent[...] = jnp.broadcast_to(bundle[...][None], sent.shape)


def receive_kernel(
    payload, weights_in, rate_in, dmat_in, acoustic_in, out,
    held, lands, rows, total, weights, rate, dmat, acoustic, one, two, arrived, left,
):
    devices, height, coarse = payload.shape
    capacity = (height - CODE_ROWS) // 3
    lines = rate.shape[1]
    part = devices // PARTS
    copies = [
        pltpu.make_async_copy(
            payload.at[k * part:(k + 1) * part], held.at[k * part:(k + 1) * part], arrived.at[k]
        )
        for k in range(PARTS)
    ]
    others = [
        pltpu.make_async_copy(src, dst, arrived.at[PARTS + k])
        for k, (src, dst) in enumerate((
            (weights_in, weights), (rate_in, rate), (dmat_in, dmat), (acoustic_in, acoustic),
        ))
    ]
    for copy in copies + others:
        copy.start()
    per = 128 // capacity
    tiles = part // per
    slots = part * capacity
    is_one, zero = jnp.bfloat16(1), jnp.bfloat16(0)
    row16 = lax.broadcasted_iota(jnp.int32, (16, slots), 0)
    for k, copy in enumerate(copies):
        copy.wait()
        mine = held.at[k * part:(k + 1) * part]
        slot = k % 2
        codes = codes_of(mine, capacity).astype(jnp.int32)
        phases = f32(codes % PHASES)
        phases = jnp.concatenate([phases, jnp.zeros((128 - tiles, 128), jnp.float32)], axis=0).T
        target = in_one_row(f32(codes // PHASES - lines // 2))
        target = jnp.broadcast_to(target, (16, slots)).astype(jnp.bfloat16)
        for n in range(lines // 16):
            line = f32(row16 + (16 * n - lines // 2)).astype(jnp.bfloat16)
            lands[slot, 16 * n:16 * (n + 1), :] = jnp.where(target == line, is_one, zero)
        for n in range(tiles):
            phase = jnp.broadcast_to(phases[:, n:n + 1], (128, coarse)).astype(jnp.bfloat16)
            for c in range(3):
                values = mine[n * per:(n + 1) * per, c * capacity:(c + 1) * capacity, :]
                values = values.reshape(128, coarse)
                for o in range(PHASES):
                    at = (c * PHASES + o) * coarse
                    rows[slot, 128 * n:128 * (n + 1), at:at + coarse] = jnp.where(
                        phase == jnp.bfloat16(o), values, zero
                    )
        landed = jnp.dot(lands[slot], rows[slot], preferred_element_type=jnp.float32)
        total[...] = landed if k == 0 else total[...] + landed
    for copy in others:
        copy.wait()
    deep = PHASES * coarse
    for c in range(3):
        gathered = total[:, c * deep:(c + 1) * deep].astype(jnp.bfloat16)
        rate[c + 1] -= jnp.dot(gathered, weights[...], preferred_element_type=jnp.float32)
    for c, value in homogeneous(rate, dmat, dx_rounded):
        one[c] = rate[c] + FIRST * value
    for c, value in homogeneous(one, dmat, dx_rounded):
        two[c] = rate[c] + SECOND * value
    leave = []
    for c, value in homogeneous(two, dmat, dx_rounded):
        one[c] = acoustic[c] + STEP * (rate[c] + THIRD * value)
        leave.append(pltpu.make_async_copy(one.at[c], out.at[c], left.at[c]))
        leave[-1].start()
    for copy in leave:
        copy.wait()


def call(kernel, name, inputs, outputs, smem=0):
    return pl.pallas_call(
        kernel,
        out_shape=outputs,
        in_specs=[scalars()] * smem + whole(len(inputs) - smem),
        out_specs=jax.tree.map(lambda _: whole(1)[0], outputs),
        compiler_params=pltpu.CompilerParams(vmem_limit_bytes=VMEM_LIMIT),
        name=name,
    )(*inputs)


def shifted(x, by):
    peers = lax.axis_size("ac")
    pairs = [(i, i + by) for i in range(peers) if 0 <= i + by < peers]
    return lax.ppermute(x, "ac", pairs)


def local(velocity, vorticity, cover, target_line, phase, fringe, acoustic):
    devices = lax.axis_size("les") * lax.axis_size("ac")
    slabs, coarse = velocity.shape[1:]
    lines, cells = acoustic.shape[1:]
    capacity = 2 * slabs * cover.shape[1] // devices
    me = lax.axis_index("les") * lax.axis_size("ac") + lax.axis_index("ac")
    place = (me % (128 // capacity)).reshape(1)

    exact = derivative_matrix(cells)
    high = exact.astype(np.float32).astype(jnp.bfloat16)
    rest = (exact - high.astype(np.float64)).astype(np.float32).astype(jnp.bfloat16)
    dmat = jnp.asarray(np.concatenate([high, rest], axis=1))
    weights = jnp.asarray(lagrange_weights(coarse, cells).astype(jnp.bfloat16))

    state_type = jax.ShapeDtypeStruct(acoustic.shape, jnp.float32)

    def donor(column):
        rows = lax.dynamic_slice_in_dim(acoustic, fringe[0, column], 1, 1)[:, 0]
        return jnp.stack([rows[0], rows[2]])

    ghosts = (shifted(donor(0), 1), shifted(donor(1), -1))
    payload = pack(
        place, velocity, vorticity, cover.T, target_line.T, phase.T, devices, capacity
    )
    payload = lax.all_to_all(payload, AXES, split_axis=0, concat_axis=0, tiled=True)
    rate, near = call(
        start_kernel, "start", (fringe, acoustic, *ghosts, dmat),
        (state_type, jax.ShapeDtypeStruct((48, cells), jnp.float32)), smem=1,
    )
    peers = lax.axis_size("ac")
    sent = pl.pallas_call(
        functools.partial(donors_kernel, lines),
        out_shape=jax.ShapeDtypeStruct((peers, 16, cells), jnp.float32),
        in_specs=[scalars()] + whole(1) + far(3),
        out_specs=whole(1)[0],
        scratch_shapes=[
            pltpu.VMEM((devices * capacity, 2 * coarse), jnp.bfloat16),
            pltpu.VMEM((16, cells), jnp.float32),
            pltpu.VMEM(weights.shape, weights.dtype),
            pltpu.VMEM(near.shape, near.dtype),
            pltpu.VMEM(dmat.shape, dmat.dtype),
            pltpu.SemaphoreType.DMA((3,)),
        ],
        compiler_params=pltpu.CompilerParams(vmem_limit_bytes=DONORS_LIMIT),
        name="donors",
    )(fringe, payload, weights, near, dmat)
    got = lax.all_to_all(sent, "ac", split_axis=0, concat_axis=0, tiled=True)
    part = devices // PARTS * capacity
    inside = pl.pallas_call(
        receive_kernel,
        out_shape=state_type,
        in_specs=far(5),
        out_specs=far(1)[0],
        scratch_shapes=[
            pltpu.VMEM(payload.shape, payload.dtype),
            pltpu.VMEM((2, lines, part), jnp.bfloat16),
            pltpu.VMEM((2, part, 3 * PHASES * coarse), jnp.bfloat16),
            pltpu.VMEM((lines, 3 * PHASES * coarse), jnp.float32),
            pltpu.VMEM(weights.shape, weights.dtype),
            pltpu.VMEM(acoustic.shape, jnp.float32),
            pltpu.VMEM(dmat.shape, dmat.dtype),
            pltpu.VMEM(acoustic.shape, jnp.float32),
            pltpu.VMEM(acoustic.shape, jnp.float32),
            pltpu.VMEM(acoustic.shape, jnp.float32),
            pltpu.SemaphoreType.DMA((PARTS + 4,)),
            pltpu.SemaphoreType.DMA((4,)),
        ],
        compiler_params=pltpu.CompilerParams(vmem_limit_bytes=VMEM_LIMIT),
        name="receive",
    )(payload, weights, rate, dmat, acoustic)
    return add_edges(inside, dmat, got, lax.axis_index("ac").reshape(1))


def solution(mesh):
    split_rows = P(None, AXES, None)
    pairs = P(AXES, None)
    return jax.shard_map(
        local,
        mesh=mesh,
        in_specs=(split_rows, split_rows, pairs, pairs, pairs, pairs, split_rows),
        out_specs=split_rows,
        check_vma=False,
    )
```

```python
import functools

import jax
import jax.numpy as jnp
import numpy as np
from jax import lax
from jax.experimental import pallas as pl
from jax.experimental.pallas import tpu as pltpu
from jax.sharding import PartitionSpec as P

PHASES = 4
ADVECT = 0.5
STEP = 0.4
AXES = ("les", "ac")
CODE_ROWS = 8
GROUP = 16
PARTS = 2
MIB = 1 << 20
VMEM_LIMIT = 60 * MIB
DONORS_LIMIT = 52000 << 10
EDGES_LIMIT = 32 * MIB
WINDOW = 5


def lagrange_weights(coarse, fine):
    table = np.zeros((PHASES, coarse, fine), np.float32)
    for phase in range(PHASES):
        numerator = PHASES * np.arange(fine) + phase
        first_tap = np.clip(numerator // (2 * PHASES) - 1, 0, coarse - 4)
        where_x = numerator.astype(np.float32) / np.float32(2 * PHASES)
        for tap in range(4):
            weight = np.ones((fine,), np.float32)
            for other in range(4):
                if other != tap:
                    gap = where_x - (first_tap + other).astype(np.float32)
                    weight = weight * gap / np.float32(tap - other)
            table[phase, first_tap + tap, np.arange(fine)] += weight
    return table.reshape(PHASES * coarse, fine)


def derivative_matrix(cells):
    off = np.eye(cells, k=1)
    a = np.eye(cells) + 0.25 * (off + off.T)
    b = 0.75 * (off - off.T)
    return np.linalg.solve(a, b).T


def whole(count):
    return [pl.BlockSpec(memory_space=pltpu.VMEM)] * count


def far(count):
    return [pl.BlockSpec(memory_space=pltpu.HBM)] * count


def scalars():
    return pl.BlockSpec(memory_space=pltpu.SMEM)


def f32(x):
    return x.astype(jnp.float32)


def pack_kernel(
    place, velocity, vorticity, cover, line, phase, payload_out,
    payload, table, ranks, vel, vor, cov, lin, pha, arrived, left,
):
    devices = payload.shape[0]
    slabs = vel.shape[1]
    coarse = vel.shape[2]
    capacity = (payload.shape[1] - CODE_ROWS) // 3
    copies = [
        pltpu.make_async_copy(src, dst, arrived.at[n])
        for n, (src, dst) in enumerate(
            ((cover, cov), (line, lin), (phase, pha), (velocity, vel), (vorticity, vor))
        )
    ]
    for copy in copies:
        copy.start()

    copies[0].wait()
    first_block, second_block = cov[0:1, :], cov[1:2, :]
    ids = lax.broadcasted_iota(jnp.int32, (devices, slabs), 0)
    hit = (first_block == ids) | (second_block == ids)
    hit_f = jnp.where(hit, 1.0, 0.0)
    width = 256
    earlier = (
        lax.broadcasted_iota(jnp.int32, (width, width), 0)
        < lax.broadcasted_iota(jnp.int32, (width, width), 1)
    )
    earlier = jnp.where(earlier, 1.0, 0.0).astype(jnp.bfloat16)
    before = jnp.zeros((devices, 1), jnp.float32)
    for k in range(slabs // width):
        part = hit_f[:, k * width:(k + 1) * width]
        rank = jnp.dot(part.astype(jnp.bfloat16), earlier, preferred_element_type=jnp.float32)
        ranks[:, k * width:(k + 1) * width] = jnp.where(part > 0.0, rank + before, -1.0)
        before = before + jnp.sum(part, axis=1, keepdims=True)

    copies[1].wait()
    copies[2].wait()
    code = lin[...] * PHASES + pha[...]
    high = f32((code // 8) * 8)
    low = f32(code % 8)
    row8 = lax.broadcasted_iota(jnp.int32, (128, slabs), 0)
    facts = jnp.where(row8 == 0, high[0:1], 0.0)
    facts = jnp.where(row8 == 1, low[0:1], facts)
    facts = jnp.where(row8 == 2, high[1:2], facts)
    facts = jnp.where(row8 == 3, low[1:2], facts)
    facts = jnp.where(row8 == 4, f32(first_block), facts)
    table[:, 3 * coarse:] = facts.T.astype(jnp.bfloat16)

    copies[3].wait()
    copies[4].wait()
    for c in range(3):
        a, b = (c + 1) % 3, (c + 2) % 3
        lamb = f32(vor[a]) * f32(vel[b]) - f32(vor[b]) * f32(vel[a])
        table[:, c * coarse:(c + 1) * coarse] = lamb.astype(jnp.bfloat16)

    rows16 = lax.broadcasted_iota(jnp.int32, (16, slabs), 0)
    slots = [f32(rows16 + start).astype(jnp.bfloat16) for start in range(0, capacity, 16)]
    one, zero = jnp.bfloat16(1), jnp.bfloat16(0)
    span = GROUP * capacity
    lane_owner = lax.broadcasted_iota(jnp.int32, (1, span), 1) // capacity
    own_lanes = (
        lax.broadcasted_iota(jnp.int32, (GROUP, span), 1) // capacity
        == lax.broadcasted_iota(jnp.int32, (GROUP, span), 0)
    )
    my_part = lax.broadcasted_iota(jnp.int32, (GROUP, 128), 1) // capacity == place[0]
    which_row = lax.broadcasted_iota(jnp.int32, (GROUP, CODE_ROWS, 128), 1)

    def spread(values):
        rows = jnp.where(own_lanes, jnp.broadcast_to(values, (GROUP, span)), 0.0)
        total = rows[:, :128]
        for k in range(1, span // 128):
            total = total + rows[:, k * 128:(k + 1) * 128]
        shift = 64
        while shift >= capacity:
            total = total + pltpu.roll(total, shift, 1)
            shift //= 2
        return jnp.where(my_part, total, 0.0)[:, None, :]

    def group(g, carry):
        first = pl.multiple_of(g * GROUP, GROUP)
        mine = ranks[pl.ds(first, GROUP), :]
        pieces = []
        for n in range(GROUP):
            row = jnp.broadcast_to(mine[n:n + 1, :], (16, slabs)).astype(jnp.bfloat16)
            pieces += [jnp.where(row == slot, one, zero) for slot in slots]
        choose = jnp.concatenate(pieces, axis=0)
        picked = jnp.dot(choose, table[...], preferred_element_type=jnp.float32)
        for c in range(3):
            rows = picked[:, c * coarse:(c + 1) * coarse].reshape(GROUP, capacity, coarse)
            payload[pl.ds(first, GROUP), c * capacity:(c + 1) * capacity, :] = rows.astype(
                jnp.bfloat16
            )
        codes = picked[:, 3 * coarse:].T
        is_first = codes[4:5] == f32(lane_owner + first)
        upper = spread(jnp.where(is_first, codes[0:1], codes[2:3]))
        lower = spread(jnp.where(is_first, codes[1:2], codes[3:4]))
        tile = jnp.where(which_row == 0, upper, jnp.where(which_row == 1, lower, 0.0))
        payload[pl.ds(first, GROUP), 3 * capacity:, :] = tile.astype(jnp.bfloat16)
        leave(g).start()
        return carry

    def leave(g):
        mine = pl.ds(pl.multiple_of(g * GROUP, GROUP), GROUP)
        return pltpu.make_async_copy(payload.at[mine], payload_out.at[mine], left.at[g])

    def gone(g, carry):
        leave(g).wait()
        return carry

    lax.fori_loop(0, devices // GROUP, group, 0, unroll=True)
    lax.fori_loop(0, devices // GROUP, gone, 0)


def pack(place, velocity, vorticity, cover, line, phase, devices, capacity):
    _, slabs, coarse = velocity.shape
    return pl.pallas_call(
        pack_kernel,
        out_shape=jax.ShapeDtypeStruct((devices, 3 * capacity + CODE_ROWS, coarse), jnp.bfloat16),
        in_specs=[scalars()] + far(5),
        out_specs=far(1)[0],
        scratch_shapes=[
            pltpu.VMEM((devices, 3 * capacity + CODE_ROWS, coarse), jnp.bfloat16),
            pltpu.VMEM((slabs, 3 * coarse + 128), jnp.bfloat16),
            pltpu.VMEM((devices, slabs), jnp.float32),
            pltpu.VMEM(velocity.shape, velocity.dtype),
            pltpu.VMEM(vorticity.shape, vorticity.dtype),
            pltpu.VMEM(cover.shape, cover.dtype),
            pltpu.VMEM(line.shape, line.dtype),
            pltpu.VMEM(phase.shape, phase.dtype),
            pltpu.SemaphoreType.DMA((5,)),
            pltpu.SemaphoreType.DMA((devices // GROUP,)),
        ],
        compiler_params=pltpu.CompilerParams(vmem_limit_bytes=VMEM_LIMIT),
        name="pack",
    )(place, velocity, vorticity, cover, line, phase)


def split(x):
    high = x.astype(jnp.bfloat16)
    return high, (x - f32(high)).astype(jnp.bfloat16)


def dx(field, dmat):
    high, low = split(field)
    cells = field.shape[-1]
    both = jnp.dot(high, dmat[...], preferred_element_type=jnp.float32)
    return (
        both[:, :cells]
        + both[:, cells:]
        + jnp.dot(low, dmat[:, :cells], preferred_element_type=jnp.float32)
    )


def dx_rounded(field, dmat):
    return jnp.dot(
        field.astype(jnp.bfloat16), dmat[:, :field.shape[-1]], preferred_element_type=jnp.float32
    )


def dy_inside(field):
    lines = field.shape[0]
    at = lax.broadcasted_iota(jnp.int32, field.shape, 0)
    above = jnp.where(at == lines - 1, 0.0, pltpu.roll(field, lines - 1, 0))
    below = jnp.where(at == 0, 0.0, pltpu.roll(field, 1, 0))
    return (above - below) * 0.5


def homogeneous(state, dmat, dx=dx):
    field = [state[c][...] for c in range(4)]
    dx_p, dx_u = dx(field[0], dmat), dx(field[1], dmat)
    yield 0, -ADVECT * dx_p - dx_u - dy_inside(field[2])
    yield 1, -ADVECT * dx_u - dx_p
    yield 2, -ADVECT * dx(field[2], dmat) - dy_inside(field[0])
    yield 3, -ADVECT * dx(field[3], dmat)


def start_kernel(fringe, state, low_ghost, high_ghost, dmat, out, near):
    lines, cells = state.shape[1:]
    for c, value in homogeneous(state, dmat):
        out[c] = value
    for c, n in ((0, 1), (2, 0)):
        out[c, 0:1, :] += 0.5 * low_ghost[n:n + 1]
        out[c, lines - 1:lines, :] -= 0.5 * high_ghost[n:n + 1]
    near[...] = jnp.zeros_like(near)
    for n in range(2):
        for c in range(3):
            for k in range(WINDOW):
                line = fringe[0, n] + (k - 2)
                row = out[c, pl.ds(jnp.clip(line, 0, lines - 1), 1), :]
                at = (n * 3 + c) * 8 + k
                near[at:at + 1, :] = jnp.where((line >= 0) & (line < lines), row, 0.0)


FIRST, SECOND, THIRD = STEP / 4, STEP / 3, STEP / 2


def edge_kernel(lines, peers, here_at, got, dmat, inside, out, fix):
    me = here_at[0]

    def bundle(by):
        exists = (me + by >= 0) & (me + by < peers)
        return jnp.where(exists, got[jnp.clip(me + by, 0, peers - 1)], 0.0)

    def pair(sent, level, column):
        first = 4 * level + 2 * column
        return sent[first:first + 1, :], sent[first + 1:first + 2, :]

    def at(sent, column, line):
        return sent[12 + column:13 + column, :] == float(line + 1)

    def first_change(sign, ghost):
        p, v = ghost
        return 0.5 * sign * FIRST * v, 0.5 * sign * FIRST * p

    def second_level(sent, column, low, high):
        p, v = pair(sent, 1, column)
        for sign, line, ghost in ((1, 0, low), (-1, lines - 1, high)):
            dp, dv = first_change(sign, ghost)
            here = at(sent, column, line)
            p, v = p + jnp.where(here, dp, 0.0), v + jnp.where(here, dv, 0.0)
        return p, v

    @pl.when(pl.program_id(0) == 0)
    def _():
        mine, back1, back2, back3 = (bundle(-n) for n in range(4))
        next1, next2, next3 = (bundle(n) for n in range(1, 4))
        up0, up1, up2 = pair(mine, 0, 0), pair(back1, 0, 0), pair(back2, 0, 0)
        down0, down1, down2 = pair(mine, 0, 1), pair(next1, 0, 1), pair(next2, 0, 1)
        up3, down3 = pair(back3, 0, 0), pair(next3, 0, 1)
        second_up = [
            second_level(mine, 0, up1, down1),
            second_level(back1, 0, up2, down0),
            second_level(back2, 0, up3, pair(back1, 0, 1)),
        ]
        second_down = [
            second_level(mine, 1, up1, down1),
            second_level(next1, 1, up0, down2),
            second_level(next2, 1, pair(next1, 0, 0), down3),
        ]
        ends = [
            (1, up1, second_up[1]), (-1, down1, second_down[1]),
            (1, up2, second_up[2]), (-1, down0, second_down[0]),
            (1, up0, second_up[0]), (-1, down2, second_down[2]),
        ]
        changes = [first_change(sign, ghost) for sign, ghost, _ in ends]
        slopes = dx(jnp.concatenate([x for pv in changes for x in pv] + [jnp.zeros_like(up0[0])] * 4), dmat)
        seconds = []
        for n, (sign, _, ghost) in enumerate(ends):
            dp, dv = changes[n]
            sp, sv = slopes[2 * n:2 * n + 1], slopes[2 * n + 1:2 * n + 2]
            edge = (
                SECOND * (-ADVECT * sp + 0.5 * sign * ghost[1]),
                SECOND * -sp,
                SECOND * (-ADVECT * sv + 0.5 * sign * ghost[0]),
            )
            seconds.append((edge, (0.5 * SECOND * sign * dv, 0.5 * SECOND * sign * dp)))

        def third_level(sent, column, low, high):
            p, v = pair(sent, 2, column)
            for line, step, (edge, inner) in ((0, 1, low), (lines - 1, -1, high)):
                for where, dp, dv in ((line, edge[0], edge[2]), (line + step, *inner)):
                    here = at(sent, column, where)
                    p, v = p + jnp.where(here, dp, 0.0), v + jnp.where(here, dv, 0.0)
            return p, v

        ghosts = (
            third_level(back1, 0, seconds[2], seconds[3]),
            third_level(next1, 1, seconds[4], seconds[5]),
        )
        rows = [x for edge, inner in seconds[:2] for x in (*edge, *inner)]
        slopes = dx(jnp.concatenate(rows + [jnp.zeros_like(rows[0])] * 6), dmat)
        for n, sign in enumerate((1, -1)):
            (p0, u0, v0), (p1, v1) = seconds[n]
            sp0, su0, sv0, sp1, sv1 = (slopes[5 * n + k:5 * n + k + 1] for k in range(5))
            half = 0.5 * sign
            ghost_p, ghost_v = ghosts[n]
            change = (
                (-ADVECT * sp0 - su0 - half * v1 + half * ghost_v, -ADVECT * sp1 + half * v0, half * v1),
                (-ADVECT * su0 - sp0, -sp1, jnp.zeros_like(p0)),
                (-ADVECT * sv0 - half * p1 + half * ghost_p, -ADVECT * sv1 + half * p0, half * p1),
            )
            fix[n] = jnp.zeros(fix.shape[1:], fix.dtype)
            for c in range(3):
                for k in range(3):
                    row = k if n == 0 else 7 - k
                    fix[n, c, row:row + 1, :] = STEP * THIRD * change[c][k]

    out[...] = inside[...] + fix[pl.program_id(0)]


def add_edges(inside, dmat, got, here_at):
    fields, lines, cells = inside.shape
    block = pl.BlockSpec((fields, 8, cells), lambda i: (0, i * (lines // 8 - 1), 0))
    return pl.pallas_call(
        functools.partial(edge_kernel, lines, got.shape[0]),
        out_shape=jax.ShapeDtypeStruct(inside.shape, inside.dtype),
        grid=(2,),
        in_specs=[scalars()] + whole(2) + [block],
        out_specs=block,
        scratch_shapes=[pltpu.VMEM((2, fields, 8, cells), jnp.float32)],
        input_output_aliases={3: 0},
        compiler_params=pltpu.CompilerParams(vmem_limit_bytes=EDGES_LIMIT),
        name="edges",
    )(here_at, got, dmat, inside)


def codes_of(payload, capacity):
    per = 128 // capacity
    codes = f32(payload[:, 3 * capacity:, :])
    codes = codes.reshape(payload.shape[0] // per, per, CODE_ROWS, 128).sum(axis=1)
    return codes.sum(axis=1)


def in_one_row(values):
    return jnp.concatenate([values[n:n + 1, :] for n in range(values.shape[0])], axis=1)


def donors_kernel(
    lines, fringe, payload, weights_in, near_in, dmat_in, sent,
    rows, bundle, weights, near_rows, dmat, arrived,
):
    copies = [
        pltpu.make_async_copy(src, dst, arrived.at[k])
        for k, (src, dst) in enumerate(
            ((weights_in, weights), (near_in, near_rows), (dmat_in, dmat))
        )
    ]
    for copy in copies:
        copy.start()
    devices, height, coarse = payload.shape
    capacity = (height - CODE_ROWS) // 3
    slots = devices * capacity
    cells = weights.shape[1]
    codes = in_one_row(codes_of(payload, capacity))
    for c in range(2):
        rows[:, c * coarse:(c + 1) * coarse] = payload[
            :, c * capacity:(c + 1) * capacity, :
        ].reshape(slots, coarse)
    for copy in copies:
        copy.wait()
    side = 24
    at = lax.broadcasted_iota(jnp.int32, (2 * side, 1), 0)
    base = jnp.where(at < side, fringe[0, 0], fringe[0, 1])
    combo = f32((base - 2) * PHASES + at % side)
    lands = jnp.where(codes == combo, 1.0, 0.0).astype(jnp.bfloat16)
    gathered = jnp.dot(lands, rows[...], preferred_element_type=jnp.float32)
    source = jnp.zeros((4 * side, cells), jnp.float32)
    both = jnp.concatenate([gathered[:, :coarse], gathered[:, coarse:]], axis=0)
    phase = lax.broadcasted_iota(jnp.int32, both.shape, 0) % PHASES
    for o in range(PHASES):
        chosen = jnp.where(phase == o, both, 0.0).astype(jnp.bfloat16)
        source += jnp.dot(
            chosen, weights[o * coarse:(o + 1) * coarse, :], preferred_element_type=jnp.float32
        )
    source = source.reshape(4 * side // PHASES, PHASES, cells).sum(axis=1)

    def rate_row(n, c, k):
        first = (n * 3 + c) * 8 + k
        row = near_rows[first:first + 1, :]
        if c > 0:
            first = (c - 1) * 2 * side // PHASES + n * side // PHASES + k
            row = row - source[first:first + 1]
        return row

    blank = jnp.zeros((1, cells), jnp.float32)
    near = [[[rate_row(n, c, k) for k in range(WINDOW)] for c in range(3)] for n in range(2)]
    slopes = [near[n][c][k] for n in range(2) for c in range(3) for k in (1, 2, 3)]
    slopes = dx(jnp.concatenate(slopes + [blank] * 6, axis=0), dmat)
    stage = []
    for n in range(2):
        p, u, v = near[n]
        dp, du, dv = (
            [slopes[9 * n + 3 * c + k:9 * n + 3 * c + k + 1] for k in range(3)] for c in range(3)
        )
        stage.append([[], [], []])
        for k in range(3):
            line = fringe[0, n] + k - 1
            real = (line >= 0) & (line < lines)
            change = (
                -ADVECT * dp[k] - du[k] - 0.5 * (v[k + 2] - v[k]),
                -ADVECT * du[k] - dp[k],
                -ADVECT * dv[k] - 0.5 * (p[k + 2] - p[k]),
            )
            for c in range(3):
                value = near[n][c][k + 1] + FIRST * change[c]
                stage[n][c].append(jnp.where(real, value, 0.0))
    slopes = [stage[n][c][1] for n in range(2) for c in range(3)]
    slopes = dx(jnp.concatenate(slopes + [blank] * 2, axis=0), dmat)
    for n in range(2):
        p, _, v = stage[n]
        dp, du, dv = (slopes[3 * n + c:3 * n + c + 1] for c in range(3))
        last_p = near[n][0][2] + SECOND * (-ADVECT * dp - du - 0.5 * (v[2] - v[0]))
        last_v = near[n][2][2] + SECOND * (-ADVECT * dv - 0.5 * (p[2] - p[0]))
        levels = (near[n][0][2], near[n][2][2]), (p[1], v[1]), (last_p, last_v)
        for level, pair in enumerate(levels):
            for k in range(2):
                at = 4 * level + 2 * n + k
                bundle[at:at + 1, :] = pair[k]
        bundle[12 + n:13 + n, :] = jnp.full((1, cells), (fringe[0, n] + 1).astype(jnp.float32))
        bundle[14 + n:15 + n, :] = blank
    sent[...] = jnp.broadcast_to(bundle[...][None], sent.shape)


def receive_kernel(
    payload, weights_in, rate_in, dmat_in, acoustic_in, out,
    held, total, weights, rate, dmat, acoustic, one, two, arrived, left,
):
    devices, height, coarse = payload.shape
    capacity = (height - CODE_ROWS) // 3
    lines = rate.shape[1]
    part = devices // PARTS
    copies = [
        pltpu.make_async_copy(
            payload.at[k * part:(k + 1) * part], held.at[k * part:(k + 1) * part], arrived.at[k]
        )
        for k in range(PARTS)
    ]
    others = [
        pltpu.make_async_copy(src, dst, arrived.at[PARTS + k])
        for k, (src, dst) in enumerate((
            (weights_in, weights), (rate_in, rate), (dmat_in, dmat), (acoustic_in, acoustic),
        ))
    ]
    for copy in copies + others:
        copy.start()
    per = 128 // capacity
    tiles = part // per
    slots = part * capacity
    is_one, zero = jnp.bfloat16(1), jnp.bfloat16(0)
    row16 = lax.broadcasted_iota(jnp.int32, (16, slots), 0)
    for k, copy in enumerate(copies):
        copy.wait()
        mine = held.at[k * part:(k + 1) * part]
        codes = codes_of(mine, capacity).astype(jnp.int32)
        phases = f32(codes % PHASES)
        phases = jnp.concatenate([phases, jnp.zeros((128 - tiles, 128), jnp.float32)], axis=0).T
        target = in_one_row(f32(codes // PHASES - lines // 2))
        target = jnp.broadcast_to(target, (16, slots)).astype(jnp.bfloat16)
        lands = jnp.concatenate(
            [
                jnp.where(
                    target == f32(row16 + (16 * n - lines // 2)).astype(jnp.bfloat16), is_one, zero
                )
                for n in range(lines // 16)
            ],
            axis=0,
        )
        phase_of = [
            jnp.broadcast_to(phases[:, n:n + 1], (128, coarse)).astype(jnp.bfloat16)
            for n in range(tiles)
        ]

        def rows_of(c, o):
            pieces = []
            for n in range(tiles):
                values = mine[n * per:(n + 1) * per, c * capacity:(c + 1) * capacity, :]
                values = values.reshape(128, coarse)
                pieces.append(jnp.concatenate(
                    [
                        jnp.where(phase_of[n] == jnp.bfloat16(p), values, zero)
                        for p in (o, o + 1)
                    ],
                    axis=1,
                ))
            return jnp.concatenate(pieces, axis=0)

        wanted = [(c, o) for c in range(3) for o in range(0, PHASES, 2)]
        rows = rows_of(*wanted[0])
        for n, (c, o) in enumerate(wanted):
            later = rows_of(*wanted[n + 1]) if n + 1 < len(wanted) else None
            landed = jnp.dot(lands, rows, preferred_element_type=jnp.float32)
            columns = slice((c * PHASES + o) * coarse, (c * PHASES + o + 2) * coarse)
            total[:, columns] = landed if k == 0 else total[:, columns] + landed
            rows = later
    for copy in others:
        copy.wait()
    deep = PHASES * coarse
    for c in range(3):
        gathered = total[:, c * deep:(c + 1) * deep].astype(jnp.bfloat16)
        rate[c + 1] -= jnp.dot(gathered, weights[...], preferred_element_type=jnp.float32)
    for c, value in homogeneous(rate, dmat, dx_rounded):
        one[c] = rate[c] + FIRST * value
    for c, value in homogeneous(one, dmat, dx_rounded):
        two[c] = rate[c] + SECOND * value
    leave = []
    for c, value in homogeneous(two, dmat, dx_rounded):
        one[c] = acoustic[c] + STEP * (rate[c] + THIRD * value)
        leave.append(pltpu.make_async_copy(one.at[c], out.at[c], left.at[c]))
        leave[-1].start()
    for copy in leave:
        copy.wait()


def call(kernel, name, inputs, outputs, smem=0):
    return pl.pallas_call(
        kernel,
        out_shape=outputs,
        in_specs=[scalars()] * smem + whole(len(inputs) - smem),
        out_specs=jax.tree.map(lambda _: whole(1)[0], outputs),
        compiler_params=pltpu.CompilerParams(vmem_limit_bytes=52000 << 10),
        name=name,
    )(*inputs)


def shifted(x, by):
    peers = lax.axis_size("ac")
    pairs = [(i, i + by) for i in range(peers) if 0 <= i + by < peers]
    return lax.ppermute(x, "ac", pairs)


def local(velocity, vorticity, cover, target_line, phase, fringe, acoustic):
    devices = lax.axis_size("les") * lax.axis_size("ac")
    slabs, coarse = velocity.shape[1:]
    lines, cells = acoustic.shape[1:]
    capacity = 2 * slabs * cover.shape[1] // devices
    me = lax.axis_index("les") * lax.axis_size("ac") + lax.axis_index("ac")
    place = (me % (128 // capacity)).reshape(1)

    exact = derivative_matrix(cells)
    high = exact.astype(np.float32).astype(jnp.bfloat16)
    rest = (exact - high.astype(np.float64)).astype(np.float32).astype(jnp.bfloat16)
    dmat = jnp.asarray(np.concatenate([high, rest], axis=1))
    weights = jnp.asarray(lagrange_weights(coarse, cells).astype(jnp.bfloat16))

    state_type = jax.ShapeDtypeStruct(acoustic.shape, jnp.float32)

    def donor(column):
        rows = lax.dynamic_slice_in_dim(acoustic, fringe[0, column], 1, 1)[:, 0]
        return jnp.stack([rows[0], rows[2]])

    ghosts = (shifted(donor(0), 1), shifted(donor(1), -1))
    payload = pack(
        place, velocity, vorticity, cover.T, target_line.T, phase.T, devices, capacity
    )
    payload = lax.all_to_all(payload, AXES, split_axis=0, concat_axis=0, tiled=True)
    rate, near = call(
        start_kernel, "start", (fringe, acoustic, *ghosts, dmat),
        (state_type, jax.ShapeDtypeStruct((48, cells), jnp.float32)), smem=1,
    )
    peers = lax.axis_size("ac")
    sent = pl.pallas_call(
        functools.partial(donors_kernel, lines),
        out_shape=jax.ShapeDtypeStruct((peers, 16, cells), jnp.float32),
        in_specs=[scalars()] + whole(1) + far(3),
        out_specs=whole(1)[0],
        scratch_shapes=[
            pltpu.VMEM((devices * capacity, 2 * coarse), jnp.bfloat16),
            pltpu.VMEM((16, cells), jnp.float32),
            pltpu.VMEM(weights.shape, weights.dtype),
            pltpu.VMEM(near.shape, near.dtype),
            pltpu.VMEM(dmat.shape, dmat.dtype),
            pltpu.SemaphoreType.DMA((3,)),
        ],
        compiler_params=pltpu.CompilerParams(vmem_limit_bytes=DONORS_LIMIT),
        name="donors",
    )(fringe, payload, weights, near, dmat)
    got = lax.all_to_all(sent, "ac", split_axis=0, concat_axis=0, tiled=True)
    inside = pl.pallas_call(
        receive_kernel,
        out_shape=state_type,
        in_specs=far(5),
        out_specs=far(1)[0],
        scratch_shapes=[
            pltpu.VMEM(payload.shape, payload.dtype),
            pltpu.VMEM((lines, 3 * PHASES * coarse), jnp.float32),
            pltpu.VMEM(weights.shape, weights.dtype),
            pltpu.VMEM(acoustic.shape, jnp.float32),
            pltpu.VMEM(dmat.shape, dmat.dtype),
            pltpu.VMEM(acoustic.shape, jnp.float32),
            pltpu.VMEM(acoustic.shape, jnp.float32),
            pltpu.VMEM(acoustic.shape, jnp.float32),
            pltpu.SemaphoreType.DMA((PARTS + 4,)),
            pltpu.SemaphoreType.DMA((4,)),
        ],
        compiler_params=pltpu.CompilerParams(vmem_limit_bytes=VMEM_LIMIT),
        name="receive",
    )(payload, weights, rate, dmat, acoustic)
    return add_edges(inside, dmat, got, lax.axis_index("ac").reshape(1))


def solution(mesh):
    split_rows = P(None, AXES, None)
    pairs = P(AXES, None)
    return jax.shard_map(
        local,
        mesh=mesh,
        in_specs=(split_rows, split_rows, pairs, pairs, pairs, pairs, split_rows),
        out_specs=split_rows,
        check_vma=False,
    )
```

```python
import functools

import jax
import jax.numpy as jnp
import numpy as np
from jax import lax
from jax.experimental import pallas as pl
from jax.experimental.pallas import tpu as pltpu
from jax.sharding import PartitionSpec as P

PHASES = 4
ADVECT = 0.5
STEP = 0.4
AXES = ("les", "ac")
CODE_ROWS = 8
GROUP = 16
PARTS = 2
QUARTERS = 4
MIB = 1 << 20
VMEM_LIMIT = 60 * MIB
DONORS_LIMIT = 52000 << 10
EDGES_LIMIT = 32 * MIB
WINDOW = 5


def lagrange_weights(coarse, fine):
    table = np.zeros((PHASES, coarse, fine), np.float32)
    for phase in range(PHASES):
        numerator = PHASES * np.arange(fine) + phase
        first_tap = np.clip(numerator // (2 * PHASES) - 1, 0, coarse - 4)
        where_x = numerator.astype(np.float32) / np.float32(2 * PHASES)
        for tap in range(4):
            weight = np.ones((fine,), np.float32)
            for other in range(4):
                if other != tap:
                    gap = where_x - (first_tap + other).astype(np.float32)
                    weight = weight * gap / np.float32(tap - other)
            table[phase, first_tap + tap, np.arange(fine)] += weight
    return table.reshape(PHASES * coarse, fine)


def derivative_matrix(cells):
    off = np.eye(cells, k=1)
    a = np.eye(cells) + 0.25 * (off + off.T)
    b = 0.75 * (off - off.T)
    return np.linalg.solve(a, b).T


def whole(count):
    return [pl.BlockSpec(memory_space=pltpu.VMEM)] * count


def far(count):
    return [pl.BlockSpec(memory_space=pltpu.HBM)] * count


def scalars():
    return pl.BlockSpec(memory_space=pltpu.SMEM)


def f32(x):
    return x.astype(jnp.float32)


def pack_kernel(
    place, velocity, vorticity, cover, line, phase, payload_out,
    payload, table, ranks, vel, vor, cov, lin, pha, arrived, left,
):
    devices = payload.shape[0]
    slabs = vel.shape[1]
    coarse = vel.shape[2]
    capacity = (payload.shape[1] - CODE_ROWS) // 3
    copies = [
        pltpu.make_async_copy(src, dst, arrived.at[n])
        for n, (src, dst) in enumerate(
            ((cover, cov), (line, lin), (phase, pha), (velocity, vel), (vorticity, vor))
        )
    ]
    for copy in copies:
        copy.start()

    copies[0].wait()
    first_block, second_block = cov[0:1, :], cov[1:2, :]
    ids = lax.broadcasted_iota(jnp.int32, (devices, slabs), 0)
    hit = (first_block == ids) | (second_block == ids)
    hit_f = jnp.where(hit, 1.0, 0.0)
    width = 256
    earlier = (
        lax.broadcasted_iota(jnp.int32, (width, width), 0)
        < lax.broadcasted_iota(jnp.int32, (width, width), 1)
    )
    earlier = jnp.where(earlier, 1.0, 0.0).astype(jnp.bfloat16)
    before = jnp.zeros((devices, 1), jnp.float32)
    for k in range(slabs // width):
        part = hit_f[:, k * width:(k + 1) * width]
        rank = jnp.dot(part.astype(jnp.bfloat16), earlier, preferred_element_type=jnp.float32)
        ranks[:, k * width:(k + 1) * width] = jnp.where(part > 0.0, rank + before, -1.0)
        before = before + jnp.sum(part, axis=1, keepdims=True)

    copies[1].wait()
    copies[2].wait()
    code = lin[...] * PHASES + pha[...]
    high = f32((code // 8) * 8)
    low = f32(code % 8)
    row8 = lax.broadcasted_iota(jnp.int32, (128, slabs), 0)
    facts = jnp.where(row8 == 0, high[0:1], 0.0)
    facts = jnp.where(row8 == 1, low[0:1], facts)
    facts = jnp.where(row8 == 2, high[1:2], facts)
    facts = jnp.where(row8 == 3, low[1:2], facts)
    facts = jnp.where(row8 == 4, f32(first_block), facts)
    table[:, 3 * coarse:] = facts.T.astype(jnp.bfloat16)

    copies[3].wait()
    copies[4].wait()
    for c in range(3):
        a, b = (c + 1) % 3, (c + 2) % 3
        lamb = f32(vor[a]) * f32(vel[b]) - f32(vor[b]) * f32(vel[a])
        table[:, c * coarse:(c + 1) * coarse] = lamb.astype(jnp.bfloat16)

    rows16 = lax.broadcasted_iota(jnp.int32, (16, slabs), 0)
    slots = [f32(rows16 + start).astype(jnp.bfloat16) for start in range(0, capacity, 16)]
    one, zero = jnp.bfloat16(1), jnp.bfloat16(0)
    span = GROUP * capacity
    lane_owner = lax.broadcasted_iota(jnp.int32, (1, span), 1) // capacity
    own_lanes = (
        lax.broadcasted_iota(jnp.int32, (GROUP, span), 1) // capacity
        == lax.broadcasted_iota(jnp.int32, (GROUP, span), 0)
    )
    my_part = lax.broadcasted_iota(jnp.int32, (GROUP, 128), 1) // capacity == place[0]
    which_row = lax.broadcasted_iota(jnp.int32, (GROUP, CODE_ROWS, 128), 1)

    def spread(values):
        rows = jnp.where(own_lanes, jnp.broadcast_to(values, (GROUP, span)), 0.0)
        total = rows[:, :128]
        for k in range(1, span // 128):
            total = total + rows[:, k * 128:(k + 1) * 128]
        shift = 64
        while shift >= capacity:
            total = total + pltpu.roll(total, shift, 1)
            shift //= 2
        return jnp.where(my_part, total, 0.0)[:, None, :]

    def group(g, carry):
        first = pl.multiple_of(g * GROUP, GROUP)
        mine = ranks[pl.ds(first, GROUP), :]
        pieces = []
        for n in range(GROUP):
            row = jnp.broadcast_to(mine[n:n + 1, :], (16, slabs)).astype(jnp.bfloat16)
            pieces += [jnp.where(row == slot, one, zero) for slot in slots]
        choose = jnp.concatenate(pieces, axis=0)
        picked = jnp.dot(choose, table[...], preferred_element_type=jnp.float32)
        for c in range(3):
            rows = picked[:, c * coarse:(c + 1) * coarse].reshape(GROUP, capacity, coarse)
            payload[pl.ds(first, GROUP), c * capacity:(c + 1) * capacity, :] = rows.astype(
                jnp.bfloat16
            )
        codes = picked[:, 3 * coarse:].T
        is_first = codes[4:5] == f32(lane_owner + first)
        upper = spread(jnp.where(is_first, codes[0:1], codes[2:3]))
        lower = spread(jnp.where(is_first, codes[1:2], codes[3:4]))
        tile = jnp.where(which_row == 0, upper, jnp.where(which_row == 1, lower, 0.0))
        payload[pl.ds(first, GROUP), 3 * capacity:, :] = tile.astype(jnp.bfloat16)
        leave(g).start()
        return carry

    def leave(g):
        mine = pl.ds(pl.multiple_of(g * GROUP, GROUP), GROUP)
        return pltpu.make_async_copy(payload.at[mine], payload_out.at[mine], left.at[g])

    def gone(g, carry):
        leave(g).wait()
        return carry

    lax.fori_loop(0, devices // GROUP, group, 0, unroll=True)
    lax.fori_loop(0, devices // GROUP, gone, 0)


def pack(place, velocity, vorticity, cover, line, phase, devices, capacity):
    _, slabs, coarse = velocity.shape
    return pl.pallas_call(
        pack_kernel,
        out_shape=jax.ShapeDtypeStruct((devices, 3 * capacity + CODE_ROWS, coarse), jnp.bfloat16),
        in_specs=[scalars()] + far(5),
        out_specs=far(1)[0],
        scratch_shapes=[
            pltpu.VMEM((devices, 3 * capacity + CODE_ROWS, coarse), jnp.bfloat16),
            pltpu.VMEM((slabs, 3 * coarse + 128), jnp.bfloat16),
            pltpu.VMEM((devices, slabs), jnp.float32),
            pltpu.VMEM(velocity.shape, velocity.dtype),
            pltpu.VMEM(vorticity.shape, vorticity.dtype),
            pltpu.VMEM(cover.shape, cover.dtype),
            pltpu.VMEM(line.shape, line.dtype),
            pltpu.VMEM(phase.shape, phase.dtype),
            pltpu.SemaphoreType.DMA((5,)),
            pltpu.SemaphoreType.DMA((devices // GROUP,)),
        ],
        compiler_params=pltpu.CompilerParams(vmem_limit_bytes=VMEM_LIMIT),
        name="pack",
    )(place, velocity, vorticity, cover, line, phase)


def split(x):
    high = x.astype(jnp.bfloat16)
    return high, (x - f32(high)).astype(jnp.bfloat16)


def dx(field, dmat):
    high, low = split(field)
    cells = field.shape[-1]
    both = jnp.dot(high, dmat[...], preferred_element_type=jnp.float32)
    return (
        both[:, :cells]
        + both[:, cells:]
        + jnp.dot(low, dmat[:, :cells], preferred_element_type=jnp.float32)
    )


def dx_rounded(field, dmat):
    return jnp.dot(
        field.astype(jnp.bfloat16), dmat[:, :field.shape[-1]], preferred_element_type=jnp.float32
    )


def dy_inside(field):
    lines = field.shape[0]
    at = lax.broadcasted_iota(jnp.int32, field.shape, 0)
    above = jnp.where(at == lines - 1, 0.0, pltpu.roll(field, lines - 1, 0))
    below = jnp.where(at == 0, 0.0, pltpu.roll(field, 1, 0))
    return (above - below) * 0.5


def homogeneous(state, dmat, dx=dx):
    field = [state[c][...] for c in range(4)]
    dx_p, dx_u = dx(field[0], dmat), dx(field[1], dmat)
    yield 0, -ADVECT * dx_p - dx_u - dy_inside(field[2])
    yield 1, -ADVECT * dx_u - dx_p
    yield 2, -ADVECT * dx(field[2], dmat) - dy_inside(field[0])
    yield 3, -ADVECT * dx(field[3], dmat)


def start_kernel(fringe, state, dmat, out, near):
    lines, cells = state.shape[1:]
    for c, value in homogeneous(state, dmat):
        out[c] = value
    near[...] = jnp.zeros_like(near)
    for n in range(2):
        for c in range(3):
            for k in range(WINDOW):
                line = fringe[0, n] + (k - 2)
                row = out[c, pl.ds(jnp.clip(line, 0, lines - 1), 1), :]
                at = (n * 3 + c) * 8 + k
                near[at:at + 1, :] = jnp.where((line >= 0) & (line < lines), row, 0.0)


FIRST, SECOND, THIRD = STEP / 4, STEP / 3, STEP / 2


def edge_kernel(lines, peers, here_at, got, dmat, inside, out, fix):
    me = here_at[0]

    def bundle(by):
        exists = (me + by >= 0) & (me + by < peers)
        return jnp.where(exists, got[jnp.clip(me + by, 0, peers - 1)], 0.0)

    def pair(sent, level, column):
        first = 4 * level + 2 * column
        return sent[first:first + 1, :], sent[first + 1:first + 2, :]

    def at(sent, column, line):
        return sent[12 + column:13 + column, :] == float(line + 1)

    def first_change(sign, ghost):
        p, v = ghost
        return 0.5 * sign * FIRST * v, 0.5 * sign * FIRST * p

    def second_level(sent, column, low, high):
        p, v = pair(sent, 1, column)
        for sign, line, ghost in ((1, 0, low), (-1, lines - 1, high)):
            dp, dv = first_change(sign, ghost)
            here = at(sent, column, line)
            p, v = p + jnp.where(here, dp, 0.0), v + jnp.where(here, dv, 0.0)
        return p, v

    @pl.when(pl.program_id(0) == 0)
    def _():
        mine, back1, back2, back3 = (bundle(-n) for n in range(4))
        next1, next2, next3 = (bundle(n) for n in range(1, 4))
        up0, up1, up2 = pair(mine, 0, 0), pair(back1, 0, 0), pair(back2, 0, 0)
        down0, down1, down2 = pair(mine, 0, 1), pair(next1, 0, 1), pair(next2, 0, 1)
        up3, down3 = pair(back3, 0, 0), pair(next3, 0, 1)
        second_up = [
            second_level(mine, 0, up1, down1),
            second_level(back1, 0, up2, down0),
            second_level(back2, 0, up3, pair(back1, 0, 1)),
        ]
        second_down = [
            second_level(mine, 1, up1, down1),
            second_level(next1, 1, up0, down2),
            second_level(next2, 1, pair(next1, 0, 0), down3),
        ]
        ends = [
            (1, up1, second_up[1]), (-1, down1, second_down[1]),
            (1, up2, second_up[2]), (-1, down0, second_down[0]),
            (1, up0, second_up[0]), (-1, down2, second_down[2]),
        ]
        changes = [first_change(sign, ghost) for sign, ghost, _ in ends]
        slopes = dx(jnp.concatenate([x for pv in changes for x in pv] + [jnp.zeros_like(up0[0])] * 4), dmat)
        seconds = []
        for n, (sign, _, ghost) in enumerate(ends):
            dp, dv = changes[n]
            sp, sv = slopes[2 * n:2 * n + 1], slopes[2 * n + 1:2 * n + 2]
            edge = (
                SECOND * (-ADVECT * sp + 0.5 * sign * ghost[1]),
                SECOND * -sp,
                SECOND * (-ADVECT * sv + 0.5 * sign * ghost[0]),
            )
            seconds.append((edge, (0.5 * SECOND * sign * dv, 0.5 * SECOND * sign * dp)))

        def third_level(sent, column, low, high):
            p, v = pair(sent, 2, column)
            for line, step, (edge, inner) in ((0, 1, low), (lines - 1, -1, high)):
                for where, dp, dv in ((line, edge[0], edge[2]), (line + step, *inner)):
                    here = at(sent, column, where)
                    p, v = p + jnp.where(here, dp, 0.0), v + jnp.where(here, dv, 0.0)
            return p, v

        ghosts = (
            third_level(back1, 0, seconds[2], seconds[3]),
            third_level(next1, 1, seconds[4], seconds[5]),
        )
        rows = [x for edge, inner in seconds[:2] for x in (*edge, *inner)]
        slopes = dx(jnp.concatenate(rows + [jnp.zeros_like(rows[0])] * 6), dmat)
        for n, sign in enumerate((1, -1)):
            (p0, u0, v0), (p1, v1) = seconds[n]
            sp0, su0, sv0, sp1, sv1 = (slopes[5 * n + k:5 * n + k + 1] for k in range(5))
            half = 0.5 * sign
            ghost_p, ghost_v = ghosts[n]
            change = (
                (-ADVECT * sp0 - su0 - half * v1 + half * ghost_v, -ADVECT * sp1 + half * v0, half * v1),
                (-ADVECT * su0 - sp0, -sp1, jnp.zeros_like(p0)),
                (-ADVECT * sv0 - half * p1 + half * ghost_p, -ADVECT * sv1 + half * p0, half * p1),
            )
            fix[n] = jnp.zeros(fix.shape[1:], fix.dtype)
            for c in range(3):
                for k in range(3):
                    row = k if n == 0 else 7 - k
                    fix[n, c, row:row + 1, :] = STEP * THIRD * change[c][k]

    out[...] = inside[...] + fix[pl.program_id(0)]


def add_edges(inside, dmat, got, here_at):
    fields, lines, cells = inside.shape
    block = pl.BlockSpec((fields, 8, cells), lambda i: (0, i * (lines // 8 - 1), 0))
    return pl.pallas_call(
        functools.partial(edge_kernel, lines, got.shape[0]),
        out_shape=jax.ShapeDtypeStruct(inside.shape, inside.dtype),
        grid=(2,),
        in_specs=[scalars()] + whole(2) + [block],
        out_specs=block,
        scratch_shapes=[pltpu.VMEM((2, fields, 8, cells), jnp.float32)],
        input_output_aliases={3: 0},
        compiler_params=pltpu.CompilerParams(vmem_limit_bytes=EDGES_LIMIT),
        name="edges",
    )(here_at, got, dmat, inside)


def codes_of(payload, capacity):
    per = 128 // capacity
    codes = f32(payload[:, 3 * capacity:, :])
    codes = codes.reshape(payload.shape[0] // per, per, CODE_ROWS, 128).sum(axis=1)
    return codes.sum(axis=1)


def in_one_row(values):
    return jnp.concatenate([values[n:n + 1, :] for n in range(values.shape[0])], axis=1)


def donors_kernel(
    lines, fringe, low_in, high_in, payload, weights_in, near_in, dmat_in, sent,
    held, low_ghost, high_ghost, bundle, weights, near_rows, dmat, arrived, landed,
):
    copies = [
        pltpu.make_async_copy(src, dst, arrived.at[k])
        for k, (src, dst) in enumerate(
            (
                (weights_in, weights), (near_in, near_rows), (dmat_in, dmat),
                (low_in, low_ghost), (high_in, high_ghost),
            )
        )
    ]
    devices, height, coarse = payload.shape
    capacity = (height - CODE_ROWS) // 3
    cells = weights.shape[1]
    part = devices // QUARTERS
    parts = [
        pltpu.make_async_copy(
            payload.at[k * part:(k + 1) * part], held.at[k * part:(k + 1) * part], landed.at[k]
        )
        for k in range(QUARTERS)
    ]
    for copy in parts + copies:
        copy.start()
    side = 24
    at = lax.broadcasted_iota(jnp.int32, (2 * side, 1), 0)
    base = jnp.where(at < side, fringe[0, 0], fringe[0, 1])
    combo = f32((base - 2) * PHASES + at % side)
    gathered = jnp.zeros((2 * side, 2 * coarse), jnp.float32)
    for k, copy in enumerate(parts):
        copy.wait()
        mine = held.at[k * part:(k + 1) * part]
        codes = in_one_row(codes_of(mine, capacity))
        lands = jnp.where(codes == combo, 1.0, 0.0).astype(jnp.bfloat16)
        rows = [
            mine[:, c * capacity:(c + 1) * capacity, :].reshape(part * capacity, coarse)
            for c in range(2)
        ]
        gathered += jnp.dot(
            lands, jnp.concatenate(rows, axis=1), preferred_element_type=jnp.float32
        )
    for copy in copies:
        copy.wait()
    source = jnp.zeros((4 * side, cells), jnp.float32)
    both = jnp.concatenate([gathered[:, :coarse], gathered[:, coarse:]], axis=0)
    phase = lax.broadcasted_iota(jnp.int32, both.shape, 0) % PHASES
    for o in range(PHASES):
        chosen = jnp.where(phase == o, both, 0.0).astype(jnp.bfloat16)
        source += jnp.dot(
            chosen, weights[o * coarse:(o + 1) * coarse, :], preferred_element_type=jnp.float32
        )
    source = source.reshape(4 * side // PHASES, PHASES, cells).sum(axis=1)

    def rate_row(n, c, k):
        first = (n * 3 + c) * 8 + k
        row = near_rows[first:first + 1, :]
        line = fringe[0, n] + (k - 2)
        if c != 1:
            other = slice(1, 2) if c == 0 else slice(0, 1)
            row = row + jnp.where(line == 0, 0.5 * low_ghost[other, :], 0.0)
            row = row - jnp.where(line == lines - 1, 0.5 * high_ghost[other, :], 0.0)
        if c > 0:
            first = (c - 1) * 2 * side // PHASES + n * side // PHASES + k
            row = row - source[first:first + 1]
        return row

    blank = jnp.zeros((1, cells), jnp.float32)
    near = [[[rate_row(n, c, k) for k in range(WINDOW)] for c in range(3)] for n in range(2)]
    slopes = [near[n][c][k] for n in range(2) for c in range(3) for k in (1, 2, 3)]
    slopes = dx(jnp.concatenate(slopes + [blank] * 6, axis=0), dmat)
    stage = []
    for n in range(2):
        p, u, v = near[n]
        dp, du, dv = (
            [slopes[9 * n + 3 * c + k:9 * n + 3 * c + k + 1] for k in range(3)] for c in range(3)
        )
        stage.append([[], [], []])
        for k in range(3):
            line = fringe[0, n] + k - 1
            real = (line >= 0) & (line < lines)
            change = (
                -ADVECT * dp[k] - du[k] - 0.5 * (v[k + 2] - v[k]),
                -ADVECT * du[k] - dp[k],
                -ADVECT * dv[k] - 0.5 * (p[k + 2] - p[k]),
            )
            for c in range(3):
                value = near[n][c][k + 1] + FIRST * change[c]
                stage[n][c].append(jnp.where(real, value, 0.0))
    slopes = [stage[n][c][1] for n in range(2) for c in range(3)]
    slopes = dx(jnp.concatenate(slopes + [blank] * 2, axis=0), dmat)
    for n in range(2):
        p, _, v = stage[n]
        dp, du, dv = (slopes[3 * n + c:3 * n + c + 1] for c in range(3))
        last_p = near[n][0][2] + SECOND * (-ADVECT * dp - du - 0.5 * (v[2] - v[0]))
        last_v = near[n][2][2] + SECOND * (-ADVECT * dv - 0.5 * (p[2] - p[0]))
        levels = (near[n][0][2], near[n][2][2]), (p[1], v[1]), (last_p, last_v)
        for level, pair in enumerate(levels):
            for k in range(2):
                at = 4 * level + 2 * n + k
                bundle[at:at + 1, :] = pair[k]
        bundle[12 + n:13 + n, :] = jnp.full((1, cells), (fringe[0, n] + 1).astype(jnp.float32))
        bundle[14 + n:15 + n, :] = blank
    sent[...] = jnp.broadcast_to(bundle[...][None], sent.shape)


def receive_kernel(
    low_in, high_in, payload, weights_in, rate_in, dmat_in, acoustic_in, out,
    held, low_ghost, high_ghost, total, weights, rate, dmat, acoustic, one, two, arrived, left,
):
    devices, height, coarse = payload.shape
    capacity = (height - CODE_ROWS) // 3
    lines = rate.shape[1]
    part = devices // PARTS
    copies = [
        pltpu.make_async_copy(
            payload.at[k * part:(k + 1) * part], held.at[k * part:(k + 1) * part], arrived.at[k]
        )
        for k in range(PARTS)
    ]
    others = [
        pltpu.make_async_copy(src, dst, arrived.at[PARTS + k])
        for k, (src, dst) in enumerate((
            (weights_in, weights), (rate_in, rate), (dmat_in, dmat), (acoustic_in, acoustic),
            (low_in, low_ghost), (high_in, high_ghost),
        ))
    ]
    for copy in copies + others:
        copy.start()
    per = 128 // capacity
    tiles = part // per
    slots = part * capacity
    is_one, zero = jnp.bfloat16(1), jnp.bfloat16(0)
    row16 = lax.broadcasted_iota(jnp.int32, (16, slots), 0)
    for k, copy in enumerate(copies):
        copy.wait()
        mine = held.at[k * part:(k + 1) * part]
        codes = codes_of(mine, capacity).astype(jnp.int32)
        phases = f32(codes % PHASES)
        phases = jnp.concatenate([phases, jnp.zeros((128 - tiles, 128), jnp.float32)], axis=0).T
        target = in_one_row(f32(codes // PHASES - lines // 2))
        target = jnp.broadcast_to(target, (16, slots)).astype(jnp.bfloat16)
        lands = jnp.concatenate(
            [
                jnp.where(
                    target == f32(row16 + (16 * n - lines // 2)).astype(jnp.bfloat16), is_one, zero
                )
                for n in range(lines // 16)
            ],
            axis=0,
        )
        phase_of = [
            jnp.broadcast_to(phases[:, n:n + 1], (128, coarse)).astype(jnp.bfloat16)
            for n in range(tiles)
        ]

        def rows_of(c, o):
            pieces = []
            for n in range(tiles):
                values = mine[n * per:(n + 1) * per, c * capacity:(c + 1) * capacity, :]
                values = values.reshape(128, coarse)
                pieces.append(jnp.concatenate(
                    [
                        jnp.where(phase_of[n] == jnp.bfloat16(p), values, zero)
                        for p in (o, o + 1)
                    ],
                    axis=1,
                ))
            return jnp.concatenate(pieces, axis=0)

        wanted = [(c, o) for c in range(3) for o in range(0, PHASES, 2)]
        rows = rows_of(*wanted[0])
        for n, (c, o) in enumerate(wanted):
            later = rows_of(*wanted[n + 1]) if n + 1 < len(wanted) else None
            landed = jnp.dot(lands, rows, preferred_element_type=jnp.float32)
            columns = slice((c * PHASES + o) * coarse, (c * PHASES + o + 2) * coarse)
            total[:, columns] = landed if k == 0 else total[:, columns] + landed
            rows = later
    for copy in others:
        copy.wait()
    for c, n in ((0, 1), (2, 0)):
        rate[c, 0:1, :] += 0.5 * low_ghost[n:n + 1, :]
        rate[c, lines - 1:lines, :] -= 0.5 * high_ghost[n:n + 1, :]
    deep = PHASES * coarse
    for c in range(3):
        gathered = total[:, c * deep:(c + 1) * deep].astype(jnp.bfloat16)
        rate[c + 1] -= jnp.dot(gathered, weights[...], preferred_element_type=jnp.float32)
    for c, value in homogeneous(rate, dmat, dx_rounded):
        one[c] = rate[c] + FIRST * value
    for c, value in homogeneous(one, dmat, dx_rounded):
        two[c] = rate[c] + SECOND * value
    leave = []
    for c, value in homogeneous(two, dmat, dx_rounded):
        one[c] = acoustic[c] + STEP * (rate[c] + THIRD * value)
        leave.append(pltpu.make_async_copy(one.at[c], out.at[c], left.at[c]))
        leave[-1].start()
    for copy in leave:
        copy.wait()


def call(kernel, name, inputs, outputs, smem=0):
    return pl.pallas_call(
        kernel,
        out_shape=outputs,
        in_specs=[scalars()] * smem + whole(len(inputs) - smem),
        out_specs=jax.tree.map(lambda _: whole(1)[0], outputs),
        compiler_params=pltpu.CompilerParams(vmem_limit_bytes=52000 << 10),
        name=name,
    )(*inputs)


def shifted(x, by):
    peers = lax.axis_size("ac")
    pairs = [(i, i + by) for i in range(peers) if 0 <= i + by < peers]
    return lax.ppermute(x, "ac", pairs)


def local(velocity, vorticity, cover, target_line, phase, fringe, acoustic):
    devices = lax.axis_size("les") * lax.axis_size("ac")
    slabs, coarse = velocity.shape[1:]
    lines, cells = acoustic.shape[1:]
    capacity = 2 * slabs * cover.shape[1] // devices
    me = lax.axis_index("les") * lax.axis_size("ac") + lax.axis_index("ac")
    place = (me % (128 // capacity)).reshape(1)

    exact = derivative_matrix(cells)
    high = exact.astype(np.float32).astype(jnp.bfloat16)
    rest = (exact - high.astype(np.float64)).astype(np.float32).astype(jnp.bfloat16)
    dmat = jnp.asarray(np.concatenate([high, rest], axis=1))
    weights = jnp.asarray(lagrange_weights(coarse, cells).astype(jnp.bfloat16))

    state_type = jax.ShapeDtypeStruct(acoustic.shape, jnp.float32)

    def donor(column):
        rows = lax.dynamic_slice_in_dim(acoustic, fringe[0, column], 1, 1)[:, 0]
        return jnp.stack([rows[0], rows[2]])

    ghosts = (shifted(donor(0), 1), shifted(donor(1), -1))
    payload = pack(
        place, velocity, vorticity, cover.T, target_line.T, phase.T, devices, capacity
    )
    payload = lax.all_to_all(payload, AXES, split_axis=0, concat_axis=0, tiled=True)
    rate, near = call(
        start_kernel, "start", (fringe, acoustic, dmat),
        (state_type, jax.ShapeDtypeStruct((48, cells), jnp.float32)), smem=1,
    )
    peers = lax.axis_size("ac")
    sent = pl.pallas_call(
        functools.partial(donors_kernel, lines),
        out_shape=jax.ShapeDtypeStruct((peers, 16, cells), jnp.float32),
        in_specs=[scalars()] + far(6),
        out_specs=whole(1)[0],
        scratch_shapes=[
            pltpu.VMEM(payload.shape, payload.dtype),
            pltpu.VMEM((2, cells), jnp.float32),
            pltpu.VMEM((2, cells), jnp.float32),
            pltpu.VMEM((16, cells), jnp.float32),
            pltpu.VMEM(weights.shape, weights.dtype),
            pltpu.VMEM(near.shape, near.dtype),
            pltpu.VMEM(dmat.shape, dmat.dtype),
            pltpu.SemaphoreType.DMA((5,)),
            pltpu.SemaphoreType.DMA((QUARTERS,)),
        ],
        compiler_params=pltpu.CompilerParams(vmem_limit_bytes=DONORS_LIMIT),
        name="donors",
    )(fringe, *ghosts, payload, weights, near, dmat)
    got = lax.all_to_all(sent, "ac", split_axis=0, concat_axis=0, tiled=True)
    inside = pl.pallas_call(
        receive_kernel,
        out_shape=state_type,
        in_specs=far(7),
        out_specs=far(1)[0],
        scratch_shapes=[
            pltpu.VMEM(payload.shape, payload.dtype),
            pltpu.VMEM((2, cells), jnp.float32),
            pltpu.VMEM((2, cells), jnp.float32),
            pltpu.VMEM((lines, 3 * PHASES * coarse), jnp.float32),
            pltpu.VMEM(weights.shape, weights.dtype),
            pltpu.VMEM(acoustic.shape, jnp.float32),
            pltpu.VMEM(dmat.shape, dmat.dtype),
            pltpu.VMEM(acoustic.shape, jnp.float32),
            pltpu.VMEM(acoustic.shape, jnp.float32),
            pltpu.VMEM(acoustic.shape, jnp.float32),
            pltpu.SemaphoreType.DMA((PARTS + 6,)),
            pltpu.SemaphoreType.DMA((4,)),
        ],
        compiler_params=pltpu.CompilerParams(vmem_limit_bytes=VMEM_LIMIT),
        name="receive",
    )(*ghosts, payload, weights, rate, dmat, acoustic)
    return add_edges(inside, dmat, got, lax.axis_index("ac").reshape(1))


def solution(mesh):
    split_rows = P(None, AXES, None)
    pairs = P(AXES, None)
    return jax.shard_map(
        local,
        mesh=mesh,
        in_specs=(split_rows, split_rows, pairs, pairs, pairs, pairs, split_rows),
        out_specs=split_rows,
        check_vma=False,
    )
```

```python
import functools

import jax
import jax.numpy as jnp
import numpy as np
from jax import lax
from jax.experimental import pallas as pl
from jax.experimental.pallas import tpu as pltpu
from jax.sharding import PartitionSpec as P

PHASES = 4
ADVECT = 0.5
STEP = 0.4
AXES = ("les", "ac")
CODE_ROWS = 8
GROUP = 16
PARTS = 2
QUARTERS = 4
MIB = 1 << 20
VMEM_LIMIT = 60 * MIB
DONORS_LIMIT = 52000 << 10
EDGES_LIMIT = 32 * MIB
WINDOW = 5


def lagrange_weights(coarse, fine):
    table = np.zeros((PHASES, coarse, fine), np.float32)
    for phase in range(PHASES):
        numerator = PHASES * np.arange(fine) + phase
        first_tap = np.clip(numerator // (2 * PHASES) - 1, 0, coarse - 4)
        where_x = numerator.astype(np.float32) / np.float32(2 * PHASES)
        for tap in range(4):
            weight = np.ones((fine,), np.float32)
            for other in range(4):
                if other != tap:
                    gap = where_x - (first_tap + other).astype(np.float32)
                    weight = weight * gap / np.float32(tap - other)
            table[phase, first_tap + tap, np.arange(fine)] += weight
    return table.reshape(PHASES * coarse, fine)


def derivative_matrix(cells):
    off = np.eye(cells, k=1)
    a = np.eye(cells) + 0.25 * (off + off.T)
    b = 0.75 * (off - off.T)
    return np.linalg.solve(a, b).T


def whole(count):
    return [pl.BlockSpec(memory_space=pltpu.VMEM)] * count


def far(count):
    return [pl.BlockSpec(memory_space=pltpu.HBM)] * count


def scalars():
    return pl.BlockSpec(memory_space=pltpu.SMEM)


def f32(x):
    return x.astype(jnp.float32)


def pack_kernel(
    place, velocity, vorticity, cover, line, phase, payload_out,
    payload, table, ranks, vel, vor, cov, lin, pha, arrived, left,
):
    devices = payload.shape[0]
    slabs = vel.shape[1]
    coarse = vel.shape[2]
    capacity = (payload.shape[1] - CODE_ROWS) // 3
    copies = [
        pltpu.make_async_copy(src, dst, arrived.at[n])
        for n, (src, dst) in enumerate(
            ((cover, cov), (line, lin), (phase, pha), (velocity, vel), (vorticity, vor))
        )
    ]
    for copy in copies:
        copy.start()

    copies[0].wait()
    first_block, second_block = cov[0:1, :], cov[1:2, :]
    ids = lax.broadcasted_iota(jnp.int32, (devices, slabs), 0)
    hit = (first_block == ids) | (second_block == ids)
    hit_f = jnp.where(hit, 1.0, 0.0)
    width = 256
    earlier = (
        lax.broadcasted_iota(jnp.int32, (width, width), 0)
        < lax.broadcasted_iota(jnp.int32, (width, width), 1)
    )
    earlier = jnp.where(earlier, 1.0, 0.0).astype(jnp.bfloat16)
    before = jnp.zeros((devices, 1), jnp.float32)
    for k in range(slabs // width):
        part = hit_f[:, k * width:(k + 1) * width]
        rank = jnp.dot(part.astype(jnp.bfloat16), earlier, preferred_element_type=jnp.float32)
        ranks[:, k * width:(k + 1) * width] = jnp.where(part > 0.0, rank + before, -1.0)
        before = before + jnp.sum(part, axis=1, keepdims=True)

    copies[1].wait()
    copies[2].wait()
    code = lin[...] * PHASES + pha[...]
    high = f32((code // 8) * 8)
    low = f32(code % 8)
    row8 = lax.broadcasted_iota(jnp.int32, (128, slabs), 0)
    facts = jnp.where(row8 == 0, high[0:1], 0.0)
    facts = jnp.where(row8 == 1, low[0:1], facts)
    facts = jnp.where(row8 == 2, high[1:2], facts)
    facts = jnp.where(row8 == 3, low[1:2], facts)
    facts = jnp.where(row8 == 4, f32(first_block), facts)
    table[:, 3 * coarse:] = facts.T.astype(jnp.bfloat16)

    copies[3].wait()
    copies[4].wait()
    for c in range(3):
        a, b = (c + 1) % 3, (c + 2) % 3
        lamb = f32(vor[a]) * f32(vel[b]) - f32(vor[b]) * f32(vel[a])
        table[:, c * coarse:(c + 1) * coarse] = lamb.astype(jnp.bfloat16)

    rows16 = lax.broadcasted_iota(jnp.int32, (16, slabs), 0)
    slots = [f32(rows16 + start).astype(jnp.bfloat16) for start in range(0, capacity, 16)]
    one, zero = jnp.bfloat16(1), jnp.bfloat16(0)
    span = GROUP * capacity
    lane_owner = lax.broadcasted_iota(jnp.int32, (1, span), 1) // capacity
    own_lanes = (
        lax.broadcasted_iota(jnp.int32, (GROUP, span), 1) // capacity
        == lax.broadcasted_iota(jnp.int32, (GROUP, span), 0)
    )
    my_part = lax.broadcasted_iota(jnp.int32, (GROUP, 128), 1) // capacity == place[0]
    which_row = lax.broadcasted_iota(jnp.int32, (GROUP, CODE_ROWS, 128), 1)

    def spread(values):
        rows = jnp.where(own_lanes, jnp.broadcast_to(values, (GROUP, span)), 0.0)
        total = rows[:, :128]
        for k in range(1, span // 128):
            total = total + rows[:, k * 128:(k + 1) * 128]
        shift = 64
        while shift >= capacity:
            total = total + pltpu.roll(total, shift, 1)
            shift //= 2
        return jnp.where(my_part, total, 0.0)[:, None, :]

    def chosen(first):
        mine = ranks[pl.ds(first, GROUP), :]
        pieces = []
        for n in range(GROUP):
            row = jnp.broadcast_to(mine[n:n + 1, :], (16, slabs)).astype(jnp.bfloat16)
            pieces += [jnp.where(row == slot, one, zero) for slot in slots]
        return jnp.concatenate(pieces, axis=0)

    def group(g, choose):
        first = g * GROUP
        picked = jnp.dot(choose, table[...], preferred_element_type=jnp.float32)
        for c in range(3):
            rows = picked[:, c * coarse:(c + 1) * coarse].reshape(GROUP, capacity, coarse)
            payload[pl.ds(first, GROUP), c * capacity:(c + 1) * capacity, :] = rows.astype(
                jnp.bfloat16
            )
        codes = picked[:, 3 * coarse:].T
        is_first = codes[4:5] == f32(lane_owner + first)
        upper = spread(jnp.where(is_first, codes[0:1], codes[2:3]))
        lower = spread(jnp.where(is_first, codes[1:2], codes[3:4]))
        tile = jnp.where(which_row == 0, upper, jnp.where(which_row == 1, lower, 0.0))
        payload[pl.ds(first, GROUP), 3 * capacity:, :] = tile.astype(jnp.bfloat16)
        leave(g).start()

    def leave(g):
        mine = pl.ds(g * GROUP, GROUP)
        return pltpu.make_async_copy(payload.at[mine], payload_out.at[mine], left.at[g])

    def gone(g, carry):
        leave(g).wait()
        return carry

    choose = chosen(0)
    for g in range(devices // GROUP):
        later = chosen((g + 1) * GROUP) if (g + 1) * GROUP < devices else None
        group(g, choose)
        choose = later
    lax.fori_loop(0, devices // GROUP, gone, 0)


def pack(place, velocity, vorticity, cover, line, phase, devices, capacity):
    _, slabs, coarse = velocity.shape
    return pl.pallas_call(
        pack_kernel,
        out_shape=jax.ShapeDtypeStruct((devices, 3 * capacity + CODE_ROWS, coarse), jnp.bfloat16),
        in_specs=[scalars()] + far(5),
        out_specs=far(1)[0],
        scratch_shapes=[
            pltpu.VMEM((devices, 3 * capacity + CODE_ROWS, coarse), jnp.bfloat16),
            pltpu.VMEM((slabs, 3 * coarse + 128), jnp.bfloat16),
            pltpu.VMEM((devices, slabs), jnp.float32),
            pltpu.VMEM(velocity.shape, velocity.dtype),
            pltpu.VMEM(vorticity.shape, vorticity.dtype),
            pltpu.VMEM(cover.shape, cover.dtype),
            pltpu.VMEM(line.shape, line.dtype),
            pltpu.VMEM(phase.shape, phase.dtype),
            pltpu.SemaphoreType.DMA((5,)),
            pltpu.SemaphoreType.DMA((devices // GROUP,)),
        ],
        compiler_params=pltpu.CompilerParams(vmem_limit_bytes=VMEM_LIMIT),
        name="pack",
    )(place, velocity, vorticity, cover, line, phase)


def split(x):
    high = x.astype(jnp.bfloat16)
    return high, (x - f32(high)).astype(jnp.bfloat16)


def dx(field, dmat):
    high, low = split(field)
    cells = field.shape[-1]
    both = jnp.dot(high, dmat[...], preferred_element_type=jnp.float32)
    return (
        both[:, :cells]
        + both[:, cells:]
        + jnp.dot(low, dmat[:, :cells], preferred_element_type=jnp.float32)
    )


def dx_rounded(field, dmat):
    return jnp.dot(
        field.astype(jnp.bfloat16), dmat[:, :field.shape[-1]], preferred_element_type=jnp.float32
    )


def dy_inside(field):
    lines = field.shape[0]
    at = lax.broadcasted_iota(jnp.int32, field.shape, 0)
    above = jnp.where(at == lines - 1, 0.0, pltpu.roll(field, lines - 1, 0))
    below = jnp.where(at == 0, 0.0, pltpu.roll(field, 1, 0))
    return (above - below) * 0.5


def homogeneous(state, dmat, dx=dx):
    field = [state[c][...] for c in range(4)]
    dx_p, dx_u = dx(field[0], dmat), dx(field[1], dmat)
    yield 0, -ADVECT * dx_p - dx_u - dy_inside(field[2])
    yield 1, -ADVECT * dx_u - dx_p
    yield 2, -ADVECT * dx(field[2], dmat) - dy_inside(field[0])
    yield 3, -ADVECT * dx(field[3], dmat)


def start_kernel(fringe, state, dmat, out, near):
    lines, cells = state.shape[1:]
    for c, value in homogeneous(state, dmat):
        out[c] = value
    near[...] = jnp.zeros_like(near)
    for n in range(2):
        for c in range(3):
            for k in range(WINDOW):
                line = fringe[0, n] + (k - 2)
                row = out[c, pl.ds(jnp.clip(line, 0, lines - 1), 1), :]
                at = (n * 3 + c) * 8 + k
                near[at:at + 1, :] = jnp.where((line >= 0) & (line < lines), row, 0.0)


FIRST, SECOND, THIRD = STEP / 4, STEP / 3, STEP / 2


def edge_kernel(lines, peers, here_at, got, dmat, inside, out, fix):
    me = here_at[0]

    def bundle(by):
        exists = (me + by >= 0) & (me + by < peers)
        return jnp.where(exists, got[jnp.clip(me + by, 0, peers - 1)], 0.0)

    def pair(sent, level, column):
        first = 4 * level + 2 * column
        return sent[first:first + 1, :], sent[first + 1:first + 2, :]

    def at(sent, column, line):
        return sent[12 + column:13 + column, :] == float(line + 1)

    def first_change(sign, ghost):
        p, v = ghost
        return 0.5 * sign * FIRST * v, 0.5 * sign * FIRST * p

    def second_level(sent, column, low, high):
        p, v = pair(sent, 1, column)
        for sign, line, ghost in ((1, 0, low), (-1, lines - 1, high)):
            dp, dv = first_change(sign, ghost)
            here = at(sent, column, line)
            p, v = p + jnp.where(here, dp, 0.0), v + jnp.where(here, dv, 0.0)
        return p, v

    @pl.when(pl.program_id(0) == 0)
    def _():
        mine, back1, back2, back3 = (bundle(-n) for n in range(4))
        next1, next2, next3 = (bundle(n) for n in range(1, 4))
        up0, up1, up2 = pair(mine, 0, 0), pair(back1, 0, 0), pair(back2, 0, 0)
        down0, down1, down2 = pair(mine, 0, 1), pair(next1, 0, 1), pair(next2, 0, 1)
        up3, down3 = pair(back3, 0, 0), pair(next3, 0, 1)
        second_up = [
            second_level(mine, 0, up1, down1),
            second_level(back1, 0, up2, down0),
            second_level(back2, 0, up3, pair(back1, 0, 1)),
        ]
        second_down = [
            second_level(mine, 1, up1, down1),
            second_level(next1, 1, up0, down2),
            second_level(next2, 1, pair(next1, 0, 0), down3),
        ]
        ends = [
            (1, up1, second_up[1]), (-1, down1, second_down[1]),
            (1, up2, second_up[2]), (-1, down0, second_down[0]),
            (1, up0, second_up[0]), (-1, down2, second_down[2]),
        ]
        changes = [first_change(sign, ghost) for sign, ghost, _ in ends]
        slopes = dx(jnp.concatenate([x for pv in changes for x in pv] + [jnp.zeros_like(up0[0])] * 4), dmat)
        seconds = []
        for n, (sign, _, ghost) in enumerate(ends):
            dp, dv = changes[n]
            sp, sv = slopes[2 * n:2 * n + 1], slopes[2 * n + 1:2 * n + 2]
            edge = (
                SECOND * (-ADVECT * sp + 0.5 * sign * ghost[1]),
                SECOND * -sp,
                SECOND * (-ADVECT * sv + 0.5 * sign * ghost[0]),
            )
            seconds.append((edge, (0.5 * SECOND * sign * dv, 0.5 * SECOND * sign * dp)))

        def third_level(sent, column, low, high):
            p, v = pair(sent, 2, column)
            for line, step, (edge, inner) in ((0, 1, low), (lines - 1, -1, high)):
                for where, dp, dv in ((line, edge[0], edge[2]), (line + step, *inner)):
                    here = at(sent, column, where)
                    p, v = p + jnp.where(here, dp, 0.0), v + jnp.where(here, dv, 0.0)
            return p, v

        ghosts = (
            third_level(back1, 0, seconds[2], seconds[3]),
            third_level(next1, 1, seconds[4], seconds[5]),
        )
        rows = [x for edge, inner in seconds[:2] for x in (*edge, *inner)]
        slopes = dx(jnp.concatenate(rows + [jnp.zeros_like(rows[0])] * 6), dmat)
        for n, sign in enumerate((1, -1)):
            (p0, u0, v0), (p1, v1) = seconds[n]
            sp0, su0, sv0, sp1, sv1 = (slopes[5 * n + k:5 * n + k + 1] for k in range(5))
            half = 0.5 * sign
            ghost_p, ghost_v = ghosts[n]
            change = (
                (-ADVECT * sp0 - su0 - half * v1 + half * ghost_v, -ADVECT * sp1 + half * v0, half * v1),
                (-ADVECT * su0 - sp0, -sp1, jnp.zeros_like(p0)),
                (-ADVECT * sv0 - half * p1 + half * ghost_p, -ADVECT * sv1 + half * p0, half * p1),
            )
            fix[n] = jnp.zeros(fix.shape[1:], fix.dtype)
            for c in range(3):
                for k in range(3):
                    row = k if n == 0 else 7 - k
                    fix[n, c, row:row + 1, :] = STEP * THIRD * change[c][k]

    out[...] = inside[...] + fix[pl.program_id(0)]


def add_edges(inside, dmat, got, here_at):
    fields, lines, cells = inside.shape
    block = pl.BlockSpec((fields, 8, cells), lambda i: (0, i * (lines // 8 - 1), 0))
    return pl.pallas_call(
        functools.partial(edge_kernel, lines, got.shape[0]),
        out_shape=jax.ShapeDtypeStruct(inside.shape, inside.dtype),
        grid=(2,),
        in_specs=[scalars()] + whole(2) + [block],
        out_specs=block,
        scratch_shapes=[pltpu.VMEM((2, fields, 8, cells), jnp.float32)],
        input_output_aliases={3: 0},
        compiler_params=pltpu.CompilerParams(vmem_limit_bytes=EDGES_LIMIT),
        name="edges",
    )(here_at, got, dmat, inside)


def codes_of(payload, capacity):
    per = 128 // capacity
    codes = f32(payload[:, 3 * capacity:, :])
    codes = codes.reshape(payload.shape[0] // per, per, CODE_ROWS, 128).sum(axis=1)
    return codes.sum(axis=1)


def in_one_row(values):
    return jnp.concatenate([values[n:n + 1, :] for n in range(values.shape[0])], axis=1)


def donors_kernel(
    lines, fringe, low_in, high_in, payload, weights_in, near_in, dmat_in, sent,
    held, low_ghost, high_ghost, bundle, weights, near_rows, dmat, arrived, landed,
):
    copies = [
        pltpu.make_async_copy(src, dst, arrived.at[k])
        for k, (src, dst) in enumerate(
            (
                (weights_in, weights), (near_in, near_rows), (dmat_in, dmat),
                (low_in, low_ghost), (high_in, high_ghost),
            )
        )
    ]
    devices, height, coarse = payload.shape
    capacity = (height - CODE_ROWS) // 3
    cells = weights.shape[1]
    part = devices // QUARTERS
    parts = [
        pltpu.make_async_copy(
            payload.at[k * part:(k + 1) * part], held.at[k * part:(k + 1) * part], landed.at[k]
        )
        for k in range(QUARTERS)
    ]
    for copy in parts + copies:
        copy.start()
    side = 24
    at = lax.broadcasted_iota(jnp.int32, (2 * side, 1), 0)
    base = jnp.where(at < side, fringe[0, 0], fringe[0, 1])
    combo = f32((base - 2) * PHASES + at % side)
    gathered = jnp.zeros((2 * side, 2 * coarse), jnp.float32)
    for k, copy in enumerate(parts):
        copy.wait()
        mine = held.at[k * part:(k + 1) * part]
        codes = in_one_row(codes_of(mine, capacity))
        lands = jnp.where(codes == combo, 1.0, 0.0).astype(jnp.bfloat16)
        rows = [
            mine[:, c * capacity:(c + 1) * capacity, :].reshape(part * capacity, coarse)
            for c in range(2)
        ]
        gathered += jnp.dot(
            lands, jnp.concatenate(rows, axis=1), preferred_element_type=jnp.float32
        )
    for copy in copies:
        copy.wait()
    source = jnp.zeros((4 * side, cells), jnp.float32)
    both = jnp.concatenate([gathered[:, :coarse], gathered[:, coarse:]], axis=0)
    phase = lax.broadcasted_iota(jnp.int32, both.shape, 0) % PHASES
    for o in range(PHASES):
        chosen = jnp.where(phase == o, both, 0.0).astype(jnp.bfloat16)
        source += jnp.dot(
            chosen, weights[o * coarse:(o + 1) * coarse, :], preferred_element_type=jnp.float32
        )
    source = source.reshape(4 * side // PHASES, PHASES, cells).sum(axis=1)

    def rate_row(n, c, k):
        first = (n * 3 + c) * 8 + k
        row = near_rows[first:first + 1, :]
        line = fringe[0, n] + (k - 2)
        if c != 1:
            other = slice(1, 2) if c == 0 else slice(0, 1)
            row = row + jnp.where(line == 0, 0.5 * low_ghost[other, :], 0.0)
            row = row - jnp.where(line == lines - 1, 0.5 * high_ghost[other, :], 0.0)
        if c > 0:
            first = (c - 1) * 2 * side // PHASES + n * side // PHASES + k
            row = row - source[first:first + 1]
        return row

    blank = jnp.zeros((1, cells), jnp.float32)
    near = [[[rate_row(n, c, k) for k in range(WINDOW)] for c in range(3)] for n in range(2)]
    slopes = [near[n][c][k] for n in range(2) for c in range(3) for k in (1, 2, 3)]
    slopes = dx(jnp.concatenate(slopes + [blank] * 6, axis=0), dmat)
    stage = []
    for n in range(2):
        p, u, v = near[n]
        dp, du, dv = (
            [slopes[9 * n + 3 * c + k:9 * n + 3 * c + k + 1] for k in range(3)] for c in range(3)
        )
        stage.append([[], [], []])
        for k in range(3):
            line = fringe[0, n] + k - 1
            real = (line >= 0) & (line < lines)
            change = (
                -ADVECT * dp[k] - du[k] - 0.5 * (v[k + 2] - v[k]),
                -ADVECT * du[k] - dp[k],
                -ADVECT * dv[k] - 0.5 * (p[k + 2] - p[k]),
            )
            for c in range(3):
                value = near[n][c][k + 1] + FIRST * change[c]
                stage[n][c].append(jnp.where(real, value, 0.0))
    slopes = [stage[n][c][1] for n in range(2) for c in range(3)]
    slopes = dx(jnp.concatenate(slopes + [blank] * 2, axis=0), dmat)
    for n in range(2):
        p, _, v = stage[n]
        dp, du, dv = (slopes[3 * n + c:3 * n + c + 1] for c in range(3))
        last_p = near[n][0][2] + SECOND * (-ADVECT * dp - du - 0.5 * (v[2] - v[0]))
        last_v = near[n][2][2] + SECOND * (-ADVECT * dv - 0.5 * (p[2] - p[0]))
        levels = (near[n][0][2], near[n][2][2]), (p[1], v[1]), (last_p, last_v)
        for level, pair in enumerate(levels):
            for k in range(2):
                at = 4 * level + 2 * n + k
                bundle[at:at + 1, :] = pair[k]
        bundle[12 + n:13 + n, :] = jnp.full((1, cells), (fringe[0, n] + 1).astype(jnp.float32))
        bundle[14 + n:15 + n, :] = blank
    sent[...] = jnp.broadcast_to(bundle[...][None], sent.shape)


def receive_kernel(
    low_in, high_in, payload, weights_in, rate_in, dmat_in, acoustic_in, out,
    held, low_ghost, high_ghost, total, weights, rate, dmat, acoustic, one, two, arrived, left,
):
    devices, height, coarse = payload.shape
    capacity = (height - CODE_ROWS) // 3
    lines = rate.shape[1]
    part = devices // PARTS
    copies = [
        pltpu.make_async_copy(
            payload.at[k * part:(k + 1) * part], held.at[k * part:(k + 1) * part], arrived.at[k]
        )
        for k in range(PARTS)
    ]
    others = [
        pltpu.make_async_copy(src, dst, arrived.at[PARTS + k])
        for k, (src, dst) in enumerate((
            (weights_in, weights), (rate_in, rate), (dmat_in, dmat), (acoustic_in, acoustic),
            (low_in, low_ghost), (high_in, high_ghost),
        ))
    ]
    for copy in copies + others:
        copy.start()
    per = 128 // capacity
    tiles = part // per
    slots = part * capacity
    is_one, zero = jnp.bfloat16(1), jnp.bfloat16(0)
    row16 = lax.broadcasted_iota(jnp.int32, (16, slots), 0)
    for k, copy in enumerate(copies):
        copy.wait()
        mine = held.at[k * part:(k + 1) * part]
        codes = codes_of(mine, capacity).astype(jnp.int32)
        phases = f32(codes % PHASES)
        phases = jnp.concatenate([phases, jnp.zeros((128 - tiles, 128), jnp.float32)], axis=0).T
        target = in_one_row(f32(codes // PHASES - lines // 2))
        target = jnp.broadcast_to(target, (16, slots)).astype(jnp.bfloat16)
        lands = jnp.concatenate(
            [
                jnp.where(
                    target == f32(row16 + (16 * n - lines // 2)).astype(jnp.bfloat16), is_one, zero
                )
                for n in range(lines // 16)
            ],
            axis=0,
        )
        phase_of = [
            jnp.broadcast_to(phases[:, n:n + 1], (128, coarse)).astype(jnp.bfloat16)
            for n in range(tiles)
        ]

        def rows_of(c, o):
            pieces = []
            for n in range(tiles):
                values = mine[n * per:(n + 1) * per, c * capacity:(c + 1) * capacity, :]
                values = values.reshape(128, coarse)
                pieces.append(jnp.concatenate(
                    [
                        jnp.where(phase_of[n] == jnp.bfloat16(p), values, zero)
                        for p in (o, o + 1)
                    ],
                    axis=1,
                ))
            return jnp.concatenate(pieces, axis=0)

        wanted = [(c, o) for c in range(3) for o in range(0, PHASES, 2)]
        rows = rows_of(*wanted[0])
        for n, (c, o) in enumerate(wanted):
            later = rows_of(*wanted[n + 1]) if n + 1 < len(wanted) else None
            landed = jnp.dot(lands, rows, preferred_element_type=jnp.float32)
            columns = slice((c * PHASES + o) * coarse, (c * PHASES + o + 2) * coarse)
            total[:, columns] = landed if k == 0 else total[:, columns] + landed
            rows = later
    for copy in others:
        copy.wait()
    for c, n in ((0, 1), (2, 0)):
        rate[c, 0:1, :] += 0.5 * low_ghost[n:n + 1, :]
        rate[c, lines - 1:lines, :] -= 0.5 * high_ghost[n:n + 1, :]
    deep = PHASES * coarse
    for c in range(3):
        gathered = total[:, c * deep:(c + 1) * deep].astype(jnp.bfloat16)
        rate[c + 1] -= jnp.dot(gathered, weights[...], preferred_element_type=jnp.float32)
    for c, value in homogeneous(rate, dmat, dx_rounded):
        one[c] = rate[c] + FIRST * value
    for c, value in homogeneous(one, dmat, dx_rounded):
        two[c] = rate[c] + SECOND * value
    leave = []
    for c, value in homogeneous(two, dmat, dx_rounded):
        one[c] = acoustic[c] + STEP * (rate[c] + THIRD * value)
        leave.append(pltpu.make_async_copy(one.at[c], out.at[c], left.at[c]))
        leave[-1].start()
    for copy in leave:
        copy.wait()


def call(kernel, name, inputs, outputs, smem=0):
    return pl.pallas_call(
        kernel,
        out_shape=outputs,
        in_specs=[scalars()] * smem + whole(len(inputs) - smem),
        out_specs=jax.tree.map(lambda _: whole(1)[0], outputs),
        compiler_params=pltpu.CompilerParams(vmem_limit_bytes=52000 << 10),
        name=name,
    )(*inputs)


def shifted(x, by):
    peers = lax.axis_size("ac")
    pairs = [(i, i + by) for i in range(peers) if 0 <= i + by < peers]
    return lax.ppermute(x, "ac", pairs)


def local(velocity, vorticity, cover, target_line, phase, fringe, acoustic):
    devices = lax.axis_size("les") * lax.axis_size("ac")
    slabs, coarse = velocity.shape[1:]
    lines, cells = acoustic.shape[1:]
    capacity = 2 * slabs * cover.shape[1] // devices
    me = lax.axis_index("les") * lax.axis_size("ac") + lax.axis_index("ac")
    place = (me % (128 // capacity)).reshape(1)

    exact = derivative_matrix(cells)
    high = exact.astype(np.float32).astype(jnp.bfloat16)
    rest = (exact - high.astype(np.float64)).astype(np.float32).astype(jnp.bfloat16)
    dmat = jnp.asarray(np.concatenate([high, rest], axis=1))
    weights = jnp.asarray(lagrange_weights(coarse, cells).astype(jnp.bfloat16))

    state_type = jax.ShapeDtypeStruct(acoustic.shape, jnp.float32)

    def donor(column):
        rows = lax.dynamic_slice_in_dim(acoustic, fringe[0, column], 1, 1)[:, 0]
        return jnp.stack([rows[0], rows[2]])

    ghosts = (shifted(donor(0), 1), shifted(donor(1), -1))
    payload = pack(
        place, velocity, vorticity, cover.T, target_line.T, phase.T, devices, capacity
    )
    payload = lax.all_to_all(payload, AXES, split_axis=0, concat_axis=0, tiled=True)
    rate, near = call(
        start_kernel, "start", (fringe, acoustic, dmat),
        (state_type, jax.ShapeDtypeStruct((48, cells), jnp.float32)), smem=1,
    )
    peers = lax.axis_size("ac")
    sent = pl.pallas_call(
        functools.partial(donors_kernel, lines),
        out_shape=jax.ShapeDtypeStruct((peers, 16, cells), jnp.float32),
        in_specs=[scalars()] + far(6),
        out_specs=whole(1)[0],
        scratch_shapes=[
            pltpu.VMEM(payload.shape, payload.dtype),
            pltpu.VMEM((2, cells), jnp.float32),
            pltpu.VMEM((2, cells), jnp.float32),
            pltpu.VMEM((16, cells), jnp.float32),
            pltpu.VMEM(weights.shape, weights.dtype),
            pltpu.VMEM(near.shape, near.dtype),
            pltpu.VMEM(dmat.shape, dmat.dtype),
            pltpu.SemaphoreType.DMA((5,)),
            pltpu.SemaphoreType.DMA((QUARTERS,)),
        ],
        compiler_params=pltpu.CompilerParams(vmem_limit_bytes=DONORS_LIMIT),
        name="donors",
    )(fringe, *ghosts, payload, weights, near, dmat)
    got = lax.all_to_all(sent, "ac", split_axis=0, concat_axis=0, tiled=True)
    inside = pl.pallas_call(
        receive_kernel,
        out_shape=state_type,
        in_specs=far(7),
        out_specs=far(1)[0],
        scratch_shapes=[
            pltpu.VMEM(payload.shape, payload.dtype),
            pltpu.VMEM((2, cells), jnp.float32),
            pltpu.VMEM((2, cells), jnp.float32),
            pltpu.VMEM((lines, 3 * PHASES * coarse), jnp.float32),
            pltpu.VMEM(weights.shape, weights.dtype),
            pltpu.VMEM(acoustic.shape, jnp.float32),
            pltpu.VMEM(dmat.shape, dmat.dtype),
            pltpu.VMEM(acoustic.shape, jnp.float32),
            pltpu.VMEM(acoustic.shape, jnp.float32),
            pltpu.VMEM(acoustic.shape, jnp.float32),
            pltpu.SemaphoreType.DMA((PARTS + 6,)),
            pltpu.SemaphoreType.DMA((4,)),
        ],
        compiler_params=pltpu.CompilerParams(vmem_limit_bytes=VMEM_LIMIT),
        name="receive",
    )(*ghosts, payload, weights, rate, dmat, acoustic)
    return add_edges(inside, dmat, got, lax.axis_index("ac").reshape(1))


def solution(mesh):
    split_rows = P(None, AXES, None)
    pairs = P(AXES, None)
    return jax.shard_map(
        local,
        mesh=mesh,
        in_specs=(split_rows, split_rows, pairs, pairs, pairs, pairs, split_rows),
        out_specs=split_rows,
        check_vma=False,
    )
```

```python
import functools

import jax
import jax.numpy as jnp
import numpy as np
from jax import lax
from jax.experimental import pallas as pl
from jax.experimental.pallas import tpu as pltpu
from jax.sharding import PartitionSpec as P

PHASES = 4
ADVECT = 0.5
STEP = 0.4
AXES = ("les", "ac")
CODE_ROWS = 8
GROUP = 16
PARTS = 2
QUARTERS = 8
MIB = 1 << 20
VMEM_LIMIT = 60 * MIB
DONORS_LIMIT = 52000 << 10
EDGES_LIMIT = 32 * MIB
WINDOW = 5


def lagrange_weights(coarse, fine):
    table = np.zeros((PHASES, coarse, fine), np.float32)
    for phase in range(PHASES):
        numerator = PHASES * np.arange(fine) + phase
        first_tap = np.clip(numerator // (2 * PHASES) - 1, 0, coarse - 4)
        where_x = numerator.astype(np.float32) / np.float32(2 * PHASES)
        for tap in range(4):
            weight = np.ones((fine,), np.float32)
            for other in range(4):
                if other != tap:
                    gap = where_x - (first_tap + other).astype(np.float32)
                    weight = weight * gap / np.float32(tap - other)
            table[phase, first_tap + tap, np.arange(fine)] += weight
    return table.reshape(PHASES * coarse, fine)


def derivative_matrix(cells):
    off = np.eye(cells, k=1)
    a = np.eye(cells) + 0.25 * (off + off.T)
    b = 0.75 * (off - off.T)
    return np.linalg.solve(a, b).T


def whole(count):
    return [pl.BlockSpec(memory_space=pltpu.VMEM)] * count


def far(count):
    return [pl.BlockSpec(memory_space=pltpu.HBM)] * count


def scalars():
    return pl.BlockSpec(memory_space=pltpu.SMEM)


def f32(x):
    return x.astype(jnp.float32)


def pack_kernel(
    place, velocity, vorticity, cover, line, phase, payload_out,
    payload, table, ranks, vel, vor, cov, lin, pha, arrived, left,
):
    devices = payload.shape[0]
    slabs = vel.shape[1]
    coarse = vel.shape[2]
    capacity = (payload.shape[1] - CODE_ROWS) // 3
    copies = [
        pltpu.make_async_copy(src, dst, arrived.at[n])
        for n, (src, dst) in enumerate(
            ((cover, cov), (line, lin), (phase, pha), (velocity, vel), (vorticity, vor))
        )
    ]
    for copy in copies:
        copy.start()

    copies[0].wait()
    first_block, second_block = cov[0:1, :], cov[1:2, :]
    ids = lax.broadcasted_iota(jnp.int32, (devices, slabs), 0)
    hit = (first_block == ids) | (second_block == ids)
    hit_f = jnp.where(hit, 1.0, 0.0)
    width = 256
    earlier = (
        lax.broadcasted_iota(jnp.int32, (width, width), 0)
        < lax.broadcasted_iota(jnp.int32, (width, width), 1)
    )
    earlier = jnp.where(earlier, 1.0, 0.0).astype(jnp.bfloat16)
    before = jnp.zeros((devices, 1), jnp.float32)
    for k in range(slabs // width):
        part = hit_f[:, k * width:(k + 1) * width]
        rank = jnp.dot(part.astype(jnp.bfloat16), earlier, preferred_element_type=jnp.float32)
        ranks[:, k * width:(k + 1) * width] = jnp.where(part > 0.0, rank + before, -1.0)
        before = before + jnp.sum(part, axis=1, keepdims=True)

    copies[1].wait()
    copies[2].wait()
    code = lin[...] * PHASES + pha[...]
    high = f32((code // 8) * 8)
    low = f32(code % 8)
    row8 = lax.broadcasted_iota(jnp.int32, (128, slabs), 0)
    facts = jnp.where(row8 == 0, high[0:1], 0.0)
    facts = jnp.where(row8 == 1, low[0:1], facts)
    facts = jnp.where(row8 == 2, high[1:2], facts)
    facts = jnp.where(row8 == 3, low[1:2], facts)
    facts = jnp.where(row8 == 4, f32(first_block), facts)
    table[:, 3 * coarse:] = facts.T.astype(jnp.bfloat16)

    copies[3].wait()
    copies[4].wait()
    for c in range(3):
        a, b = (c + 1) % 3, (c + 2) % 3
        lamb = f32(vor[a]) * f32(vel[b]) - f32(vor[b]) * f32(vel[a])
        table[:, c * coarse:(c + 1) * coarse] = lamb.astype(jnp.bfloat16)

    rows16 = lax.broadcasted_iota(jnp.int32, (16, slabs), 0)
    slots = [f32(rows16 + start).astype(jnp.bfloat16) for start in range(0, capacity, 16)]
    one, zero = jnp.bfloat16(1), jnp.bfloat16(0)
    span = GROUP * capacity
    lane_owner = lax.broadcasted_iota(jnp.int32, (1, span), 1) // capacity
    own_lanes = (
        lax.broadcasted_iota(jnp.int32, (GROUP, span), 1) // capacity
        == lax.broadcasted_iota(jnp.int32, (GROUP, span), 0)
    )
    my_part = lax.broadcasted_iota(jnp.int32, (GROUP, 128), 1) // capacity == place[0]
    which_row = lax.broadcasted_iota(jnp.int32, (GROUP, CODE_ROWS, 128), 1)

    def spread(values):
        rows = jnp.where(own_lanes, jnp.broadcast_to(values, (GROUP, span)), 0.0)
        total = rows[:, :128]
        for k in range(1, span // 128):
            total = total + rows[:, k * 128:(k + 1) * 128]
        shift = 64
        while shift >= capacity:
            total = total + pltpu.roll(total, shift, 1)
            shift //= 2
        return jnp.where(my_part, total, 0.0)[:, None, :]

    def group(g, carry):
        first = pl.multiple_of(g * GROUP, GROUP)
        mine = ranks[pl.ds(first, GROUP), :]
        pieces = []
        for n in range(GROUP):
            row = jnp.broadcast_to(mine[n:n + 1, :], (16, slabs)).astype(jnp.bfloat16)
            pieces += [jnp.where(row == slot, one, zero) for slot in slots]
        choose = jnp.concatenate(pieces, axis=0)
        picked = jnp.dot(choose, table[...], preferred_element_type=jnp.float32)
        for c in range(3):
            rows = picked[:, c * coarse:(c + 1) * coarse].reshape(GROUP, capacity, coarse)
            payload[pl.ds(first, GROUP), c * capacity:(c + 1) * capacity, :] = rows.astype(
                jnp.bfloat16
            )
        codes = picked[:, 3 * coarse:].T
        is_first = codes[4:5] == f32(lane_owner + first)
        upper = spread(jnp.where(is_first, codes[0:1], codes[2:3]))
        lower = spread(jnp.where(is_first, codes[1:2], codes[3:4]))
        tile = jnp.where(which_row == 0, upper, jnp.where(which_row == 1, lower, 0.0))
        payload[pl.ds(first, GROUP), 3 * capacity:, :] = tile.astype(jnp.bfloat16)
        leave(g).start()
        return carry

    def leave(g):
        mine = pl.ds(pl.multiple_of(g * GROUP, GROUP), GROUP)
        return pltpu.make_async_copy(payload.at[mine], payload_out.at[mine], left.at[g])

    def gone(g, carry):
        leave(g).wait()
        return carry

    lax.fori_loop(0, devices // GROUP, group, 0, unroll=True)
    lax.fori_loop(0, devices // GROUP, gone, 0)


def pack(place, velocity, vorticity, cover, line, phase, devices, capacity):
    _, slabs, coarse = velocity.shape
    return pl.pallas_call(
        pack_kernel,
        out_shape=jax.ShapeDtypeStruct((devices, 3 * capacity + CODE_ROWS, coarse), jnp.bfloat16),
        in_specs=[scalars()] + far(5),
        out_specs=far(1)[0],
        scratch_shapes=[
            pltpu.VMEM((devices, 3 * capacity + CODE_ROWS, coarse), jnp.bfloat16),
            pltpu.VMEM((slabs, 3 * coarse + 128), jnp.bfloat16),
            pltpu.VMEM((devices, slabs), jnp.float32),
            pltpu.VMEM(velocity.shape, velocity.dtype),
            pltpu.VMEM(vorticity.shape, vorticity.dtype),
            pltpu.VMEM(cover.shape, cover.dtype),
            pltpu.VMEM(line.shape, line.dtype),
            pltpu.VMEM(phase.shape, phase.dtype),
            pltpu.SemaphoreType.DMA((5,)),
            pltpu.SemaphoreType.DMA((devices // GROUP,)),
        ],
        compiler_params=pltpu.CompilerParams(vmem_limit_bytes=VMEM_LIMIT),
        name="pack",
    )(place, velocity, vorticity, cover, line, phase)


def split(x):
    high = x.astype(jnp.bfloat16)
    return high, (x - f32(high)).astype(jnp.bfloat16)


def dx(field, dmat):
    high, low = split(field)
    cells = field.shape[-1]
    both = jnp.dot(high, dmat[...], preferred_element_type=jnp.float32)
    return (
        both[:, :cells]
        + both[:, cells:]
        + jnp.dot(low, dmat[:, :cells], preferred_element_type=jnp.float32)
    )


def dx_rounded(field, dmat):
    return jnp.dot(
        field.astype(jnp.bfloat16), dmat[:, :field.shape[-1]], preferred_element_type=jnp.float32
    )


def dy_inside(field):
    lines = field.shape[0]
    at = lax.broadcasted_iota(jnp.int32, field.shape, 0)
    above = jnp.where(at == lines - 1, 0.0, pltpu.roll(field, lines - 1, 0))
    below = jnp.where(at == 0, 0.0, pltpu.roll(field, 1, 0))
    return (above - below) * 0.5


def homogeneous(state, dmat, dx=dx):
    field = [state[c][...] for c in range(4)]
    dx_p, dx_u = dx(field[0], dmat), dx(field[1], dmat)
    yield 0, -ADVECT * dx_p - dx_u - dy_inside(field[2])
    yield 1, -ADVECT * dx_u - dx_p
    yield 2, -ADVECT * dx(field[2], dmat) - dy_inside(field[0])
    yield 3, -ADVECT * dx(field[3], dmat)


def start_kernel(fringe, state, dmat, out, near):
    lines, cells = state.shape[1:]
    for c, value in homogeneous(state, dmat):
        out[c] = value
    near[...] = jnp.zeros_like(near)
    for n in range(2):
        for c in range(3):
            for k in range(WINDOW):
                line = fringe[0, n] + (k - 2)
                row = out[c, pl.ds(jnp.clip(line, 0, lines - 1), 1), :]
                at = (n * 3 + c) * 8 + k
                near[at:at + 1, :] = jnp.where((line >= 0) & (line < lines), row, 0.0)


FIRST, SECOND, THIRD = STEP / 4, STEP / 3, STEP / 2


def edge_kernel(lines, peers, here_at, got, dmat, inside, out, fix):
    me = here_at[0]

    def bundle(by):
        exists = (me + by >= 0) & (me + by < peers)
        return jnp.where(exists, got[jnp.clip(me + by, 0, peers - 1)], 0.0)

    def pair(sent, level, column):
        first = 4 * level + 2 * column
        return sent[first:first + 1, :], sent[first + 1:first + 2, :]

    def at(sent, column, line):
        return sent[12 + column:13 + column, :] == float(line + 1)

    def first_change(sign, ghost):
        p, v = ghost
        return 0.5 * sign * FIRST * v, 0.5 * sign * FIRST * p

    def second_level(sent, column, low, high):
        p, v = pair(sent, 1, column)
        for sign, line, ghost in ((1, 0, low), (-1, lines - 1, high)):
            dp, dv = first_change(sign, ghost)
            here = at(sent, column, line)
            p, v = p + jnp.where(here, dp, 0.0), v + jnp.where(here, dv, 0.0)
        return p, v

    @pl.when(pl.program_id(0) == 0)
    def _():
        mine, back1, back2, back3 = (bundle(-n) for n in range(4))
        next1, next2, next3 = (bundle(n) for n in range(1, 4))
        up0, up1, up2 = pair(mine, 0, 0), pair(back1, 0, 0), pair(back2, 0, 0)
        down0, down1, down2 = pair(mine, 0, 1), pair(next1, 0, 1), pair(next2, 0, 1)
        up3, down3 = pair(back3, 0, 0), pair(next3, 0, 1)
        second_up = [
            second_level(mine, 0, up1, down1),
            second_level(back1, 0, up2, down0),
            second_level(back2, 0, up3, pair(back1, 0, 1)),
        ]
        second_down = [
            second_level(mine, 1, up1, down1),
            second_level(next1, 1, up0, down2),
            second_level(next2, 1, pair(next1, 0, 0), down3),
        ]
        ends = [
            (1, up1, second_up[1]), (-1, down1, second_down[1]),
            (1, up2, second_up[2]), (-1, down0, second_down[0]),
            (1, up0, second_up[0]), (-1, down2, second_down[2]),
        ]
        changes = [first_change(sign, ghost) for sign, ghost, _ in ends]
        slopes = dx(jnp.concatenate([x for pv in changes for x in pv] + [jnp.zeros_like(up0[0])] * 4), dmat)
        seconds = []
        for n, (sign, _, ghost) in enumerate(ends):
            dp, dv = changes[n]
            sp, sv = slopes[2 * n:2 * n + 1], slopes[2 * n + 1:2 * n + 2]
            edge = (
                SECOND * (-ADVECT * sp + 0.5 * sign * ghost[1]),
                SECOND * -sp,
                SECOND * (-ADVECT * sv + 0.5 * sign * ghost[0]),
            )
            seconds.append((edge, (0.5 * SECOND * sign * dv, 0.5 * SECOND * sign * dp)))

        def third_level(sent, column, low, high):
            p, v = pair(sent, 2, column)
            for line, step, (edge, inner) in ((0, 1, low), (lines - 1, -1, high)):
                for where, dp, dv in ((line, edge[0], edge[2]), (line + step, *inner)):
                    here = at(sent, column, where)
                    p, v = p + jnp.where(here, dp, 0.0), v + jnp.where(here, dv, 0.0)
            return p, v

        ghosts = (
            third_level(back1, 0, seconds[2], seconds[3]),
            third_level(next1, 1, seconds[4], seconds[5]),
        )
        rows = [x for edge, inner in seconds[:2] for x in (*edge, *inner)]
        slopes = dx(jnp.concatenate(rows + [jnp.zeros_like(rows[0])] * 6), dmat)
        for n, sign in enumerate((1, -1)):
            (p0, u0, v0), (p1, v1) = seconds[n]
            sp0, su0, sv0, sp1, sv1 = (slopes[5 * n + k:5 * n + k + 1] for k in range(5))
            half = 0.5 * sign
            ghost_p, ghost_v = ghosts[n]
            change = (
                (-ADVECT * sp0 - su0 - half * v1 + half * ghost_v, -ADVECT * sp1 + half * v0, half * v1),
                (-ADVECT * su0 - sp0, -sp1, jnp.zeros_like(p0)),
                (-ADVECT * sv0 - half * p1 + half * ghost_p, -ADVECT * sv1 + half * p0, half * p1),
            )
            fix[n] = jnp.zeros(fix.shape[1:], fix.dtype)
            for c in range(3):
                for k in range(3):
                    row = k if n == 0 else 7 - k
                    fix[n, c, row:row + 1, :] = STEP * THIRD * change[c][k]

    out[...] = inside[...] + fix[pl.program_id(0)]


def add_edges(inside, dmat, got, here_at):
    fields, lines, cells = inside.shape
    block = pl.BlockSpec((fields, 8, cells), lambda i: (0, i * (lines // 8 - 1), 0))
    return pl.pallas_call(
        functools.partial(edge_kernel, lines, got.shape[0]),
        out_shape=jax.ShapeDtypeStruct(inside.shape, inside.dtype),
        grid=(2,),
        in_specs=[scalars()] + whole(2) + [block],
        out_specs=block,
        scratch_shapes=[pltpu.VMEM((2, fields, 8, cells), jnp.float32)],
        input_output_aliases={3: 0},
        compiler_params=pltpu.CompilerParams(vmem_limit_bytes=EDGES_LIMIT),
        name="edges",
    )(here_at, got, dmat, inside)


def codes_of(payload, capacity):
    per = 128 // capacity
    codes = f32(payload[:, 3 * capacity:, :])
    codes = codes.reshape(payload.shape[0] // per, per, CODE_ROWS, 128).sum(axis=1)
    return codes.sum(axis=1)


def in_one_row(values):
    return jnp.concatenate([values[n:n + 1, :] for n in range(values.shape[0])], axis=1)


def donors_kernel(
    lines, fringe, low_in, high_in, payload, weights_in, near_in, dmat_in, sent,
    held, low_ghost, high_ghost, bundle, weights, near_rows, dmat, arrived, landed,
):
    copies = [
        pltpu.make_async_copy(src, dst, arrived.at[k])
        for k, (src, dst) in enumerate(
            (
                (weights_in, weights), (near_in, near_rows), (dmat_in, dmat),
                (low_in, low_ghost), (high_in, high_ghost),
            )
        )
    ]
    devices, height, coarse = payload.shape
    capacity = (height - CODE_ROWS) // 3
    cells = weights.shape[1]
    part = devices // QUARTERS
    parts = [
        pltpu.make_async_copy(
            payload.at[k * part:(k + 1) * part], held.at[k * part:(k + 1) * part], landed.at[k]
        )
        for k in range(QUARTERS)
    ]
    for copy in parts + copies:
        copy.start()
    side = 24
    at = lax.broadcasted_iota(jnp.int32, (2 * side, 1), 0)
    base = jnp.where(at < side, fringe[0, 0], fringe[0, 1])
    combo = f32((base - 2) * PHASES + at % side)
    gathered = jnp.zeros((2 * side, 2 * coarse), jnp.float32)
    for k, copy in enumerate(parts):
        copy.wait()
        mine = held.at[k * part:(k + 1) * part]
        codes = in_one_row(codes_of(mine, capacity))
        lands = jnp.where(codes == combo, 1.0, 0.0).astype(jnp.bfloat16)
        rows = [
            mine[:, c * capacity:(c + 1) * capacity, :].reshape(part * capacity, coarse)
            for c in range(2)
        ]
        gathered += jnp.dot(
            lands, jnp.concatenate(rows, axis=1), preferred_element_type=jnp.float32
        )
    for copy in copies:
        copy.wait()
    source = jnp.zeros((4 * side, cells), jnp.float32)
    both = jnp.concatenate([gathered[:, :coarse], gathered[:, coarse:]], axis=0)
    phase = lax.broadcasted_iota(jnp.int32, both.shape, 0) % PHASES
    for o in range(PHASES):
        chosen = jnp.where(phase == o, both, 0.0).astype(jnp.bfloat16)
        source += jnp.dot(
            chosen, weights[o * coarse:(o + 1) * coarse, :], preferred_element_type=jnp.float32
        )
    source = source.reshape(4 * side // PHASES, PHASES, cells).sum(axis=1)

    def rate_row(n, c, k):
        first = (n * 3 + c) * 8 + k
        row = near_rows[first:first + 1, :]
        line = fringe[0, n] + (k - 2)
        if c != 1:
            other = slice(1, 2) if c == 0 else slice(0, 1)
            row = row + jnp.where(line == 0, 0.5 * low_ghost[other, :], 0.0)
            row = row - jnp.where(line == lines - 1, 0.5 * high_ghost[other, :], 0.0)
        if c > 0:
            first = (c - 1) * 2 * side // PHASES + n * side // PHASES + k
            row = row - source[first:first + 1]
        return row

    blank = jnp.zeros((1, cells), jnp.float32)
    near = [[[rate_row(n, c, k) for k in range(WINDOW)] for c in range(3)] for n in range(2)]
    slopes = [near[n][c][k] for n in range(2) for c in range(3) for k in (1, 2, 3)]
    slopes = dx(jnp.concatenate(slopes + [blank] * 6, axis=0), dmat)
    stage = []
    for n in range(2):
        p, u, v = near[n]
        dp, du, dv = (
            [slopes[9 * n + 3 * c + k:9 * n + 3 * c + k + 1] for k in range(3)] for c in range(3)
        )
        stage.append([[], [], []])
        for k in range(3):
            line = fringe[0, n] + k - 1
            real = (line >= 0) & (line < lines)
            change = (
                -ADVECT * dp[k] - du[k] - 0.5 * (v[k + 2] - v[k]),
                -ADVECT * du[k] - dp[k],
                -ADVECT * dv[k] - 0.5 * (p[k + 2] - p[k]),
            )
            for c in range(3):
                value = near[n][c][k + 1] + FIRST * change[c]
                stage[n][c].append(jnp.where(real, value, 0.0))
    slopes = [stage[n][c][1] for n in range(2) for c in range(3)]
    slopes = dx(jnp.concatenate(slopes + [blank] * 2, axis=0), dmat)
    for n in range(2):
        p, _, v = stage[n]
        dp, du, dv = (slopes[3 * n + c:3 * n + c + 1] for c in range(3))
        last_p = near[n][0][2] + SECOND * (-ADVECT * dp - du - 0.5 * (v[2] - v[0]))
        last_v = near[n][2][2] + SECOND * (-ADVECT * dv - 0.5 * (p[2] - p[0]))
        levels = (near[n][0][2], near[n][2][2]), (p[1], v[1]), (last_p, last_v)
        for level, pair in enumerate(levels):
            for k in range(2):
                at = 4 * level + 2 * n + k
                bundle[at:at + 1, :] = pair[k]
        bundle[12 + n:13 + n, :] = jnp.full((1, cells), (fringe[0, n] + 1).astype(jnp.float32))
        bundle[14 + n:15 + n, :] = blank
    sent[...] = jnp.broadcast_to(bundle[...][None], sent.shape)


def receive_kernel(
    low_in, high_in, payload, weights_in, rate_in, dmat_in, acoustic_in, out,
    held, low_ghost, high_ghost, total, weights, rate, dmat, acoustic, one, two, arrived, left,
):
    devices, height, coarse = payload.shape
    capacity = (height - CODE_ROWS) // 3
    lines = rate.shape[1]
    part = devices // PARTS
    copies = [
        pltpu.make_async_copy(
            payload.at[k * part:(k + 1) * part], held.at[k * part:(k + 1) * part], arrived.at[k]
        )
        for k in range(PARTS)
    ]
    others = [
        pltpu.make_async_copy(src, dst, arrived.at[PARTS + k])
        for k, (src, dst) in enumerate((
            (weights_in, weights), (rate_in, rate), (dmat_in, dmat), (acoustic_in, acoustic),
            (low_in, low_ghost), (high_in, high_ghost),
        ))
    ]
    for copy in copies + others:
        copy.start()
    per = 128 // capacity
    tiles = part // per
    slots = part * capacity
    is_one, zero = jnp.bfloat16(1), jnp.bfloat16(0)
    row16 = lax.broadcasted_iota(jnp.int32, (16, slots), 0)
    for k, copy in enumerate(copies):
        copy.wait()
        mine = held.at[k * part:(k + 1) * part]
        codes = codes_of(mine, capacity).astype(jnp.int32)
        phases = f32(codes % PHASES)
        phases = jnp.concatenate([phases, jnp.zeros((128 - tiles, 128), jnp.float32)], axis=0).T
        target = in_one_row(f32(codes // PHASES - lines // 2))
        target = jnp.broadcast_to(target, (16, slots)).astype(jnp.bfloat16)
        lands = jnp.concatenate(
            [
                jnp.where(
                    target == f32(row16 + (16 * n - lines // 2)).astype(jnp.bfloat16), is_one, zero
                )
                for n in range(lines // 16)
            ],
            axis=0,
        )
        phase_of = [
            jnp.broadcast_to(phases[:, n:n + 1], (128, coarse)).astype(jnp.bfloat16)
            for n in range(tiles)
        ]

        def rows_of(c, o):
            pieces = []
            for n in range(tiles):
                values = mine[n * per:(n + 1) * per, c * capacity:(c + 1) * capacity, :]
                values = values.reshape(128, coarse)
                pieces.append(jnp.concatenate(
                    [
                        jnp.where(phase_of[n] == jnp.bfloat16(p), values, zero)
                        for p in (o, o + 1)
                    ],
                    axis=1,
                ))
            return jnp.concatenate(pieces, axis=0)

        wanted = [(c, o) for c in range(3) for o in range(0, PHASES, 2)]
        rows = rows_of(*wanted[0])
        for n, (c, o) in enumerate(wanted):
            later = rows_of(*wanted[n + 1]) if n + 1 < len(wanted) else None
            landed = jnp.dot(lands, rows, preferred_element_type=jnp.float32)
            columns = slice((c * PHASES + o) * coarse, (c * PHASES + o + 2) * coarse)
            total[:, columns] = landed if k == 0 else total[:, columns] + landed
            rows = later
    for copy in others:
        copy.wait()
    for c, n in ((0, 1), (2, 0)):
        rate[c, 0:1, :] += 0.5 * low_ghost[n:n + 1, :]
        rate[c, lines - 1:lines, :] -= 0.5 * high_ghost[n:n + 1, :]
    deep = PHASES * coarse
    for c in range(3):
        gathered = total[:, c * deep:(c + 1) * deep].astype(jnp.bfloat16)
        rate[c + 1] -= jnp.dot(gathered, weights[...], preferred_element_type=jnp.float32)
    for c, value in homogeneous(rate, dmat, dx_rounded):
        one[c] = rate[c] + FIRST * value
    for c, value in homogeneous(one, dmat, dx_rounded):
        two[c] = rate[c] + SECOND * value
    leave = []
    for c, value in homogeneous(two, dmat, dx_rounded):
        one[c] = acoustic[c] + STEP * (rate[c] + THIRD * value)
        leave.append(pltpu.make_async_copy(one.at[c], out.at[c], left.at[c]))
        leave[-1].start()
    for copy in leave:
        copy.wait()


def call(kernel, name, inputs, outputs, smem=0):
    return pl.pallas_call(
        kernel,
        out_shape=outputs,
        in_specs=[scalars()] * smem + whole(len(inputs) - smem),
        out_specs=jax.tree.map(lambda _: whole(1)[0], outputs),
        compiler_params=pltpu.CompilerParams(vmem_limit_bytes=52000 << 10),
        name=name,
    )(*inputs)


def shifted(x, by):
    peers = lax.axis_size("ac")
    pairs = [(i, i + by) for i in range(peers) if 0 <= i + by < peers]
    return lax.ppermute(x, "ac", pairs)


def local(velocity, vorticity, cover, target_line, phase, fringe, acoustic):
    devices = lax.axis_size("les") * lax.axis_size("ac")
    slabs, coarse = velocity.shape[1:]
    lines, cells = acoustic.shape[1:]
    capacity = 2 * slabs * cover.shape[1] // devices
    me = lax.axis_index("les") * lax.axis_size("ac") + lax.axis_index("ac")
    place = (me % (128 // capacity)).reshape(1)

    exact = derivative_matrix(cells)
    high = exact.astype(np.float32).astype(jnp.bfloat16)
    rest = (exact - high.astype(np.float64)).astype(np.float32).astype(jnp.bfloat16)
    dmat = jnp.asarray(np.concatenate([high, rest], axis=1))
    weights = jnp.asarray(lagrange_weights(coarse, cells).astype(jnp.bfloat16))

    state_type = jax.ShapeDtypeStruct(acoustic.shape, jnp.float32)

    def donor(column):
        rows = lax.dynamic_slice_in_dim(acoustic, fringe[0, column], 1, 1)[:, 0]
        return jnp.stack([rows[0], rows[2]])

    ghosts = (shifted(donor(0), 1), shifted(donor(1), -1))
    payload = pack(
        place, velocity, vorticity, cover.T, target_line.T, phase.T, devices, capacity
    )
    payload = lax.all_to_all(payload, AXES, split_axis=0, concat_axis=0, tiled=True)
    rate, near = call(
        start_kernel, "start", (fringe, acoustic, dmat),
        (state_type, jax.ShapeDtypeStruct((48, cells), jnp.float32)), smem=1,
    )
    peers = lax.axis_size("ac")
    sent = pl.pallas_call(
        functools.partial(donors_kernel, lines),
        out_shape=jax.ShapeDtypeStruct((peers, 16, cells), jnp.float32),
        in_specs=[scalars()] + far(6),
        out_specs=whole(1)[0],
        scratch_shapes=[
            pltpu.VMEM(payload.shape, payload.dtype),
            pltpu.VMEM((2, cells), jnp.float32),
            pltpu.VMEM((2, cells), jnp.float32),
            pltpu.VMEM((16, cells), jnp.float32),
            pltpu.VMEM(weights.shape, weights.dtype),
            pltpu.VMEM(near.shape, near.dtype),
            pltpu.VMEM(dmat.shape, dmat.dtype),
            pltpu.SemaphoreType.DMA((5,)),
            pltpu.SemaphoreType.DMA((QUARTERS,)),
        ],
        compiler_params=pltpu.CompilerParams(vmem_limit_bytes=DONORS_LIMIT),
        name="donors",
    )(fringe, *ghosts, payload, weights, near, dmat)
    got = lax.all_to_all(sent, "ac", split_axis=0, concat_axis=0, tiled=True)
    inside = pl.pallas_call(
        receive_kernel,
        out_shape=state_type,
        in_specs=far(7),
        out_specs=far(1)[0],
        scratch_shapes=[
            pltpu.VMEM(payload.shape, payload.dtype),
            pltpu.VMEM((2, cells), jnp.float32),
            pltpu.VMEM((2, cells), jnp.float32),
            pltpu.VMEM((lines, 3 * PHASES * coarse), jnp.float32),
            pltpu.VMEM(weights.shape, weights.dtype),
            pltpu.VMEM(acoustic.shape, jnp.float32),
            pltpu.VMEM(dmat.shape, dmat.dtype),
            pltpu.VMEM(acoustic.shape, jnp.float32),
            pltpu.VMEM(acoustic.shape, jnp.float32),
            pltpu.VMEM(acoustic.shape, jnp.float32),
            pltpu.SemaphoreType.DMA((PARTS + 6,)),
            pltpu.SemaphoreType.DMA((4,)),
        ],
        compiler_params=pltpu.CompilerParams(vmem_limit_bytes=VMEM_LIMIT),
        name="receive",
    )(*ghosts, payload, weights, rate, dmat, acoustic)
    return add_edges(inside, dmat, got, lax.axis_index("ac").reshape(1))


def solution(mesh):
    split_rows = P(None, AXES, None)
    pairs = P(AXES, None)
    return jax.shard_map(
        local,
        mesh=mesh,
        in_specs=(split_rows, split_rows, pairs, pairs, pairs, pairs, split_rows),
        out_specs=split_rows,
        check_vma=False,
    )
```
